32 devices in a mesh: sector: 8 (over y, x, core), op: 4 (over z).
Axes of the slice: x: 2, y: 2, z: 4, core: 2. Of those that a mesh axis runs over, the one named last changes fastest.
Arguments:
- theta: float32 [32, 128, 128], P('sector'), may hold values from -6 to 6
- left_env: bfloat16 [32, 64, 128, 128], P('sector', 'op'), may hold values from -3 to 3
- right_env: bfloat16 [32, 64, 128, 128], P('sector', 'op'), may hold values from -3 to 3
- perm: int32 [32], replicated, may hold values from 0 to 31, each once
- dims: int32 [32, 2], P('sector'), may hold values from 32 to 128, as said below
Outputs:
- lanczos_vec: float32 [32, 128, 128], P('sector')
- coeffs: float32 [6], replicated
- density: float32 [32, 128, 128], P('sector')
The draws below stay inside these ranges and needn't reach their ends.
Inputs may be any that keep to these rules, and one draw needn't show every extreme that they name: `dims`: each entry is a kept dimension of 32 to 128; the first position has 128 on both sides.
All inputs are finite; a program needn't handle non-finite values.
Results may differ from the reference program's by a relative error of at most 0.012.
Values may be sent and summed in bfloat16 or wider, within the bound.
A program may use at most 64 MiB of HBM per device.

```python
import math
import jax
import jax.numpy as jnp
from jax import lax

BLK = 128
SEC_DEV = 4
SECTORS = 32
TERMS = 64


def draw_dims(key, part):
    key = jax.random.fold_in(key, 7)
    values = jax.random.randint(key, (SECTORS, 2), BLK // 4, BLK + 1).astype(jnp.int32)
    return values.at[0].set(BLK)


def build_env(spread_part, group_log, block_factor):
    own_count = (TERMS + 1) // 3
    base_amp = jnp.sqrt(jnp.sqrt(jnp.float32(TERMS)) / jnp.float32(own_count))
    group_idx = jnp.arange(SECTORS, dtype=jnp.int32) // SEC_DEV
    amplitude = base_amp * jnp.exp(group_log)[group_idx] * block_factor
    own_terms = (jnp.arange(TERMS, dtype=jnp.int32) % 3 == 1).astype(jnp.float32)
    identity = jnp.eye(BLK, dtype=jnp.float32)
    diagonal = amplitude[:, None, None, None] * own_terms[None, :, None, None] * identity[None, None, :, :]
    return (spread_part / jnp.sqrt(jnp.float32(BLK)) + diagonal).astype(jnp.bfloat16)


def group_ramp(group_key, low_log, high_log):
    groups = SECTORS // SEC_DEV
    frac = jnp.arange(groups, dtype=jnp.float32) / jnp.float32(max(groups - 1, 1))
    jitter = jax.random.uniform(group_key, (groups,), jnp.float32, -0.15, 0.15)
    return low_log + (high_log - low_log) * frac + jitter


def draw_left_env(key, part):
    key = jax.random.fold_in(key, 11)
    noise_key, group_key, block_key = jax.random.split(key, 3)
    shape = (SECTORS, TERMS, BLK, BLK)
    block_factor = jax.random.uniform(block_key, (SECTORS,), jnp.float32, 0.8, 1.2)
    spread_part = jnp.clip(jax.random.normal(noise_key, shape, jnp.float32), -4.0, 4.0)
    group_log = group_ramp(group_key, math.log(0.33), 0.0)
    return build_env(spread_part, group_log, block_factor)


def draw_right_env(key, part):
    key = jax.random.fold_in(key, 13)
    noise_key, group_key, block_key = jax.random.split(key, 3)
    shape = (SECTORS, TERMS, BLK, BLK)
    block_factor = jax.random.uniform(block_key, (SECTORS,), jnp.float32, 0.8, 1.2)
    spread_part = jnp.clip(jax.random.normal(noise_key, shape, jnp.float32), -4.0, 4.0)
    group_log = group_ramp(group_key, math.log(0.33), 0.0)
    return build_env(spread_part, group_log, block_factor)


def levels(rng, shape, cuts, least, largest):
    def one(position, parts):
        steps = jax.random.uniform(jax.random.fold_in(jax.random.fold_in(rng, 6), position), (parts,), jnp.float32, least / len(cuts), largest / len(cuts))
        return jnp.repeat(jnp.exp(steps), shape[position] // parts).reshape((-1,) + (1,) * (len(shape) - position - 1))

    gain = one(*cuts[0])
    for cut in cuts[1:]:
        gain = gain * one(*cut)
    return gain


def noise(key, shape, scale, most, cuts=(), kind=jnp.bfloat16):
    drawn = scale * jax.random.normal(key, shape, jnp.float32)
    if cuts:
        drawn = drawn * levels(key, shape, cuts, -0.22, 0.18)
    return jnp.clip(drawn, -most, most).astype(kind)


def setup_inputs(seed: int = 0) -> dict:
    arg_keys = jax.random.split(jax.random.key(seed), 6)
    return {
        "theta": noise(arg_keys[0], (SECTORS, BLK, BLK), 1.0, 6.0, ((0, 8),), jnp.float32),
        "left_env": draw_left_env(jax.random.fold_in(arg_keys[5], 71), 0),
        "right_env": draw_right_env(jax.random.fold_in(arg_keys[5], 71), 0),
        "perm": jax.random.permutation(arg_keys[3], SECTORS).astype(jnp.int32),
        "dims": draw_dims(jax.random.fold_in(arg_keys[5], 71), 0),
    }


def make_mask(dims):
    rows = jnp.arange(BLK, dtype=jnp.int32)
    inside_rows = (rows[None, :] < dims[:, 0:1]).astype(jnp.float32)
    inside_cols = (rows[None, :] < dims[:, 1:2]).astype(jnp.float32)
    return inside_rows[:, :, None] * inside_cols[:, None, :]

def apply_ham(vec, left_env, right_env, perm, mask):
    pos_of = jnp.argsort(perm).astype(jnp.int32)
    vec_b = vec.astype(jnp.bfloat16)
    shifts = jnp.arange(3, dtype=jnp.int32) - 1
    term_q = jnp.arange(TERMS, dtype=jnp.int32) % 3

    def single(p):
        sector_id = perm[p]
        src = pos_of[(sector_id + shifts) % SECTORS]
        nbrs = vec_b[src].astype(jnp.float32)
        picked = nbrs[term_q]
        inner = jnp.einsum('wij,wjk->wik', left_env[p].astype(jnp.float32), picked, precision=lax.Precision.HIGHEST).astype(jnp.bfloat16)
        return jnp.einsum('wik,wkl->il', inner.astype(jnp.float32), right_env[p].astype(jnp.float32), precision=lax.Precision.HIGHEST)
    total = lax.map(single, jnp.arange(SECTORS, dtype=jnp.int32))
    return total * mask / jnp.sqrt(jnp.float32(TERMS))

def reference(theta, left_env, right_env, perm, dims):
    count = jnp.float32(SECTORS * BLK * BLK)
    mask = make_mask(dims)
    start_vec = theta * mask
    vector = start_vec / jnp.sqrt(jnp.sum(start_vec * start_vec) / count + 1e-06)
    previous = jnp.zeros_like(vector)
    beta = jnp.float32(0.0)
    alphas = []
    betas = []
    for step in range(3):
        image = apply_ham(vector, left_env, right_env, perm, mask)
        alpha = jnp.sum(vector * image) / count
        resid = image - alpha * vector - beta * previous
        beta = jnp.sqrt(jnp.sum(resid * resid) / count + 1e-06)
        previous, vector = (vector, resid / beta)
        alphas.append(alpha)
        betas.append(beta)
    coeffs = jnp.stack(alphas + betas)
    density = jnp.einsum('pij,pkj->pik', vector, vector, precision=lax.Precision.HIGHEST) / BLK
    return (vector, coeffs, density)
```

```python
import functools

import jax
import jax.numpy as jnp
from jax import lax
from jax.experimental import pallas as pl
from jax.experimental.pallas import tpu as pltpu
from jax.sharding import PartitionSpec as P

MESH = pl.DeviceIdType.MESH
F32 = jnp.float32
BF16 = jnp.bfloat16
STEPS = 3


def kernel(
    n_sec, n_op,
    theta_ref, left_hbm, right_hbm, perm_ref, dims_ref,
    vec_ref, coef_ref, dens_ref,
    left_v, right_v, gath, pb, rsb, az, ap,
    env_sem, rsem, zsend, psend, fsend, rs_send, rs_recv,
    az_send, az_recv, ap_send, ap_recv,
):
    sec_dev, width, _ = theta_ref.shape
    term_dev = left_hbm.shape[1]
    total = n_sec * sec_dev
    count = float(total * width * width)
    scale = float((term_dev * n_op) ** -0.5)
    rows = sec_dev * width // n_op
    cpb = width // rows
    n_chip = n_sec // 2
    aligned = n_op == sec_dev

    s = lax.axis_index("sector")
    z = lax.axis_index("op")
    core = lax.rem(s, 2)
    chip = s // 2
    sib = s + 1 - 2 * core
    peers = [2 * lax.rem(chip + m, n_chip) + core for m in range(1, n_chip)]
    others = [2 * lax.rem(chip + m, n_chip) + 1 - core for m in range(n_chip)]
    mates = [lax.rem(z + m, n_op) for m in range(1, n_op)]
    plane = [lax.rem(s + m, n_sec) for m in range(1, n_sec)]

    env = []
    for p in range(sec_dev):
        env.append(pltpu.make_async_copy(left_hbm.at[p], left_v.at[p], env_sem.at[0, p]))
        env.append(pltpu.make_async_copy(right_hbm.at[p], right_v.at[p], env_sem.at[1, p]))
    for copy in env:
        copy.start()

    barrier = pltpu.get_barrier_semaphore()
    for other in plane:
        pl.semaphore_signal(barrier, inc=1, device_id=(other, z), device_id_type=MESH)
    for other in mates:
        pl.semaphore_signal(barrier, inc=1, device_id=(s, other), device_id_type=MESH)

    def block_mask(p, first, n):
        r = lax.broadcasted_iota(jnp.int32, (n, width), 0) + first
        c = lax.broadcasted_iota(jnp.int32, (n, width), 1)
        return jnp.where((r < dims_ref[p, 0]) & (c < dims_ref[p, 1]), 1.0, 0.0).astype(F32)

    def chunk(ref, base, j):
        if cpb == 1:
            return ref.at[base + j]
        return ref.at[base + j // cpb, pl.ds(pl.multiple_of(lax.rem(j, cpb) * rows, rows), rows)]

    def slot(owner, j):
        return chunk(gath, owner * sec_dev, j)

    def row(owner):
        return gath.at[pl.ds(owner * sec_dev, sec_dev)]

    def send(src, dst, ssem, dsem, dev):
        copy = pltpu.make_async_remote_copy(
            src_ref=src, dst_ref=dst, send_sem=ssem, recv_sem=dsem,
            device_id=dev, device_id_type=MESH,
        )
        copy.start()
        return copy

    def arrived(dst, dsem):
        pltpu.make_async_remote_copy(
            src_ref=dst, dst_ref=dst, send_sem=zsend.at[0], recv_sem=dsem,
            device_id=(sib, z), device_id_type=MESH,
        ).wait_recv()

    def fold(x):
        return jnp.sum(x.reshape(x.shape[0] // 8, 8, width), axis=0)

    def whole(x):
        return jnp.sum(x, keepdims=True)

    own_p = z // cpb
    own_r = pl.multiple_of(lax.rem(z, cpb) * rows, rows)
    mask = block_mask(own_p, own_r, rows)
    for p in range(sec_dev):
        gath[s * sec_dev + p] = (theta_ref[p] * block_mask(p, 0, width)).astype(BF16)
    u = theta_ref[own_p, pl.ds(own_r, rows), :] * mask
    rr = fold(u * u)

    pl.semaphore_wait(barrier, n_sec - 1 + n_op - 1)

    sends = []
    for i, peer in enumerate(peers + [sib]):
        sends.append(send(row(s), row(s), psend.at[0, i], rsem.at[s, 0], (peer, z)))

    order = [lax.rem(z + 1 + i, sec_dev) if aligned else i for i in range(sec_dev)]
    wants = []
    for p in order:
        mine = perm_ref[s * sec_dev + p]
        for c in range(3):
            q = lax.rem(z * term_dev + c, 3)
            wants.append(lax.rem(mine + q - 1 + total, total))

    def look(i, found):
        here = perm_ref[i]
        return tuple(jnp.where(here == w, i, f) for w, f in zip(wants, found))

    src = lax.fori_loop(0, total, look, tuple(jnp.int32(0) for _ in wants))

    for i, peer in enumerate(peers):
        arrived(row(peer), rsem.at[peer, 0])
        sends.append(send(row(peer), row(peer), fsend.at[0, i], rsem.at[peer, 0], (sib, z)))
    for other in others:
        arrived(row(other), rsem.at[other, 0])
    for copy in env:
        copy.wait()

    def reduce_scalars(use, tiles):
        az[use, z] = tiles
        out = []
        for i, mate in enumerate(mates):
            out.append(send(az.at[use, z], az.at[use, z], az_send.at[use, i], az_recv.at[use, z], (s, mate)))
        for mate in mates:
            arrived(az.at[use, mate], az_recv.at[use, mate])
        acc = az[use, 0]
        for j in range(1, n_op):
            acc = acc + az[use, j]
        ap[use, s] = acc
        for i, other in enumerate(plane):
            out.append(send(ap.at[use, s], ap.at[use, s], ap_send.at[use, i], ap_recv.at[use, s], (other, z)))
        for other in plane:
            arrived(ap.at[use, other], ap_recv.at[use, other])
        acc = ap[use, 0]
        for j in range(1, n_sec):
            acc = acc + ap[use, j]
        for copy in out:
            copy.wait_send()
        return whole(acc[0:8]), whole(acc[8:16])

    prev = jnp.zeros_like(u)
    alphas, betas = [], []
    for step in range(STEPS):
        if step > 0:
            slot(s, z)[...] = u.astype(BF16)
            sends = []
            for i, mate in enumerate(mates):
                sends.append(send(slot(s, z), slot(s, z), zsend.at[i], rsem.at[s, z], (s, mate)))
            for m, j in enumerate([z] + mates):
                if m > 0:
                    arrived(slot(s, j), rsem.at[s, j])
                for i, peer in enumerate(peers + [sib]):
                    sends.append(send(slot(s, j), slot(s, j), psend.at[m, i], rsem.at[s, j], (peer, z)))
            for m, j in enumerate([z] + mates):
                for i, peer in enumerate(peers):
                    arrived(slot(peer, j), rsem.at[peer, j])
                    sends.append(send(slot(peer, j), slot(peer, j), fsend.at[m, i], rsem.at[peer, j], (sib, z)))
            for j in [z] + mates:
                for other in others:
                    arrived(slot(other, j), rsem.at[other, j])

        dot_acc = jnp.zeros((8, width), F32)
        rs = []
        for i, p in enumerate(order):
            inner = [None] * term_dev
            for c in range(3):
                terms = list(range(c, term_dev, 3))
                lhs = jnp.concatenate([left_v[p, t] for t in terms], axis=0)
                got = jnp.dot(lhs, gath[src[3 * i + c]], preferred_element_type=F32).astype(BF16)
                for n, t in enumerate(terms):
                    inner[t] = got[n * width:(n + 1) * width]
            part = jnp.dot(
                jnp.concatenate(inner, axis=1),
                right_v[p].reshape(term_dev * width, width),
                preferred_element_type=F32,
            )
            pb[p] = part.astype(BF16)
            dot_acc = dot_acc + fold(part * gath[s * sec_dev + p].astype(F32))
            if aligned and i < sec_dev - 1:
                rs.append(send(pb.at[p], rsb.at[z], rs_send.at[i], rs_recv.at[z], (s, p)))
        if not aligned:
            for i, mate in enumerate(mates):
                rs.append(send(chunk(pb, 0, mate), rsb.at[z], rs_send.at[i], rs_recv.at[z], (s, mate)))
        rsb[z] = chunk(pb, 0, z)[...]
        for copy in sends:
            copy.wait_send()

        a_sum, n_sum = reduce_scalars(step % 2, jnp.concatenate([dot_acc, rr], axis=0))
        norm = jnp.sqrt(n_sum / count + 1e-06)
        inv = 1.0 / norm
        alpha = a_sum * (scale / count) * inv * inv
        alphas.append(alpha)
        if step > 0:
            betas.append(norm)

        for mate in mates:
            arrived(rsb.at[mate], rs_recv.at[mate])
        image = rsb[0].astype(F32)
        for j in range(1, n_op):
            image = image + rsb[j].astype(F32)
        for copy in rs:
            copy.wait_send()
        v = u * inv
        resid = image * mask * (inv * scale) - alpha * v
        if step > 0:
            resid = resid - norm * prev
        prev, u = v, resid
        rr = fold(u * u)

    slot(s, z)[...] = u.astype(BF16)
    sends = []
    for i, mate in enumerate(mates):
        sends.append(send(slot(s, z), slot(s, z), zsend.at[i], rsem.at[s, z], (s, mate)))
    _, n_sum = reduce_scalars(STEPS % 2, jnp.concatenate([rr, rr], axis=0))
    norm = jnp.sqrt(n_sum / count + 1e-06)
    inv = 1.0 / norm
    betas.append(norm)
    lane = lax.broadcasted_iota(jnp.int32, (8, 128), 1)
    coef = jnp.zeros((8, 128), F32)
    for i, value in enumerate(alphas + betas):
        coef = jnp.where(lane == i, value, coef)
    coef_ref[...] = coef
    for mate in mates:
        arrived(slot(s, mate), rsem.at[s, mate])
    for p in range(sec_dev):
        block = gath[s * sec_dev + p]
        vec_ref[p] = block.astype(F32) * inv
        outer = lax.dot_general(block, block, (((1,), (1,)), ((), ())), preferred_element_type=F32)
        dens_ref[p] = outer * (inv * inv * (1.0 / width))
    for copy in sends:
        copy.wait_send()


def per_device(theta, left_env, right_env, perm, dims):
    sec_dev, width, _ = theta.shape
    term_dev = left_env.shape[1]
    n_sec, n_op = lax.axis_size("sector"), lax.axis_size("op")
    rows = sec_dev * width // n_op
    n_chip = n_sec // 2
    dma = pltpu.SemaphoreType.DMA
    vmem = pl.BlockSpec(memory_space=pltpu.VMEM)
    smem = pl.BlockSpec(memory_space=pltpu.SMEM)
    hbm = pl.BlockSpec(memory_space=pl.ANY)
    vec, coef, dens = pl.pallas_call(
        functools.partial(kernel, n_sec, n_op),
        out_shape=(
            jax.ShapeDtypeStruct(theta.shape, F32),
            jax.ShapeDtypeStruct((8, 128), F32),
            jax.ShapeDtypeStruct(theta.shape, F32),
        ),
        in_specs=[vmem, hbm, hbm, smem, smem],
        out_specs=(vmem, vmem, vmem),
        scratch_shapes=[
            pltpu.VMEM(left_env.shape, BF16),
            pltpu.VMEM(right_env.shape, BF16),
            pltpu.VMEM((n_sec * sec_dev, width, width), BF16),
            pltpu.VMEM((sec_dev, width, width), BF16),
            pltpu.VMEM((n_op, rows, width), BF16),
            pltpu.VMEM((2, n_op, 16, width), F32),
            pltpu.VMEM((2, n_sec, 16, width), F32),
            dma((2, sec_dev)),
            dma((n_sec, n_op)),
            dma((n_op,)),
            dma((n_op, n_chip)),
            dma((n_op, n_chip)),
            dma((n_op,)),
            dma((n_op,)),
            dma((2, n_op)),
            dma((2, n_op)),
            dma((2, n_sec)),
            dma((2, n_sec)),
        ],
        compiler_params=pltpu.CompilerParams(
            collective_id=0, has_side_effects=True, vmem_limit_bytes=40 * 1024 * 1024
        ),
        cost_estimate=pl.CostEstimate(
            flops=STEPS * 4 * sec_dev * term_dev * width**3,
            bytes_accessed=4 * sec_dev * term_dev * width**2,
            transcendentals=0,
        ),
    )(theta, left_env, right_env, perm, dims)
    return vec, coef[0, :6], dens


def solution(mesh):
    placed = (
        P("sector", None, None),
        P("sector", "op", None, None),
        P("sector", "op", None, None),
        P(),
        P("sector", None),
    )
    return jax.shard_map(
        per_device,
        mesh=mesh,
        in_specs=placed,
        out_specs=(P("sector", None, None), P(), P("sector", None, None)),
        check_vma=False,
    )
```

```python
import functools

import jax
import jax.numpy as jnp
from jax import lax
from jax.experimental import pallas as pl
from jax.experimental.pallas import tpu as pltpu
from jax.sharding import PartitionSpec as P

MESH = pl.DeviceIdType.MESH
F32 = jnp.float32
BF16 = jnp.bfloat16
STEPS = 3


def kernel(
    n_sec, n_op,
    theta_hbm, left_hbm, right_hbm, perm_ref, dims_ref,
    vec_ref, coef_ref, dens_ref,
    theta_v, left_v, right_v, gath_a, gath_b, basis, pb, rsb, az, ap,
    env_sem, rsem, zsend, psend, fsend, relay, rs_send, rs_recv,
    az_send, az_recv, ap_send, ap_recv,
):
    gath = (gath_a, gath_b)
    sec_dev, width, _ = theta_v.shape
    term_dev = left_v.shape[1]
    total = n_sec * sec_dev
    count = float(total * width * width)
    scale = float((term_dev * n_op) ** -0.5)
    rows = sec_dev * width // n_op
    cpb = width // rows
    n_chip = n_sec // 2
    aligned = n_op == sec_dev
    square = n_chip == 4

    s = lax.axis_index("sector")
    z = lax.axis_index("op")
    core = lax.rem(s, 2)
    chip = s // 2
    sib = s + 1 - 2 * core
    if square:
        beside = [chip + 1 - 2 * lax.rem(chip, 2), lax.rem(chip + 2, 4), 3 - chip]
    else:
        beside = [lax.rem(chip + m, n_chip) for m in range(1, n_chip)]
    peers = [2 * c + core for c in beside]
    direct = peers[:2] if square else peers
    others = [sib] + [2 * c + 1 - core for c in beside]
    mates = [lax.rem(z + m, n_op) for m in range(1, n_op)]
    plane = [lax.rem(s + m, n_sec) for m in range(1, n_sec)]

    fetch = pltpu.make_async_copy(theta_hbm, theta_v, env_sem.at[2, 0])
    fetch.start()
    env = []
    for p in range(sec_dev):
        env.append(pltpu.make_async_copy(left_hbm.at[p], left_v.at[p], env_sem.at[0, p]))
        env.append(pltpu.make_async_copy(right_hbm.at[p], right_v.at[p], env_sem.at[1, p]))
    for copy in env:
        copy.start()

    barrier = pltpu.get_barrier_semaphore()
    for other in plane:
        pl.semaphore_signal(barrier, inc=1, device_id=(other, z), device_id_type=MESH)
    for other in mates:
        pl.semaphore_signal(barrier, inc=1, device_id=(s, other), device_id_type=MESH)

    def block_mask(p, first, n):
        r = lax.broadcasted_iota(jnp.int32, (n, width), 0) + first
        c = lax.broadcasted_iota(jnp.int32, (n, width), 1)
        return jnp.where((r < dims_ref[p, 0]) & (c < dims_ref[p, 1]), 1.0, 0.0).astype(F32)

    def chunk(ref, base, j):
        if cpb == 1:
            return ref.at[base + j]
        return ref.at[base + j // cpb, pl.ds(pl.multiple_of(lax.rem(j, cpb) * rows, rows), rows)]

    def slot(g, owner, j):
        return chunk(gath[g], owner * sec_dev, j)

    def send(src, dst, ssem, dsem, dev):
        copy = pltpu.make_async_remote_copy(
            src_ref=src, dst_ref=dst, send_sem=ssem, recv_sem=dsem,
            device_id=dev, device_id_type=MESH,
        )
        copy.start()
        return copy

    def arrived(dst, dsem):
        pltpu.make_async_remote_copy(
            src_ref=dst, dst_ref=dst, send_sem=zsend.at[0], recv_sem=dsem,
            device_id=(sib, z), device_id_type=MESH,
        ).wait_recv()

    def fold(x):
        return jnp.sum(x.reshape(x.shape[0] // 8, 8, width), axis=0)

    def whole(x):
        return jnp.sum(x, keepdims=True)

    def move(g, j, owner, ssem, dev):
        return send(slot(g, owner, j), slot(g, owner, j), ssem, rsem.at[g, owner, j], (dev, z))

    def spread_z(g):
        return [
            send(slot(g, s, z), slot(g, s, z), zsend.at[i], rsem.at[g, s, z], (s, mate))
            for i, mate in enumerate(mates)
        ]

    def spread_plane(g, m, j):
        return [move(g, j, s, psend.at[m, i], dev) for i, dev in enumerate(direct + [sib])]

    def pass_on(g, m, j):
        out = []
        for i, peer in enumerate(peers):
            arrived(slot(g, peer, j), rsem.at[g, peer, j])
            if square and i == m % 2:
                out.append(move(g, j, peer, relay.at[m], peers[1 - i]))
            out.append(move(g, j, peer, fsend.at[m, i], sib))
        return out

    def collect(g):
        for j in [z] + mates:
            for other in others:
                arrived(slot(g, other, j), rsem.at[g, other, j])

    own_p = z // cpb
    own_r = pl.multiple_of(lax.rem(z, cpb) * rows, rows)
    mask = block_mask(own_p, own_r, rows)
    fetch.wait()
    for p in range(sec_dev):
        gath[0][s * sec_dev + p] = (theta_v[p] * block_mask(p, 0, width)).astype(BF16)

    pl.semaphore_wait(barrier, n_sec - 1 + n_op - 1)

    sends = []
    for m, j in enumerate([z] + mates):
        sends += spread_plane(0, m, j)

    order = [lax.rem(z + 1 + i, sec_dev) if aligned else i for i in range(sec_dev)]
    wants = []
    for p in order:
        mine = perm_ref[s * sec_dev + p]
        for c in range(3):
            q = lax.rem(z * term_dev + c, 3)
            wants.append(lax.rem(mine + q - 1 + total, total))
    own_c = lax.rem(3 * term_dev * n_op + 1 - z * term_dev, 3)

    def look(i, found):
        here = perm_ref[i]
        return tuple(jnp.where(here == w, i, f) for w, f in zip(wants, found))

    src = lax.fori_loop(0, total, look, tuple(jnp.int32(0) for _ in wants))

    for m, j in enumerate([z] + mates):
        sends += pass_on(0, m, j)
    collect(0)
    for copy in env:
        copy.wait()

    def share(use):
        return [
            send(az.at[use, z], az.at[use, z], az_send.at[use, i], az_recv.at[use, z], (s, mate))
            for i, mate in enumerate(mates)
        ]

    def add_op(use):
        for mate in mates:
            arrived(az.at[use, mate], az_recv.at[use, mate])
        acc = az[use, 0]
        for j in range(1, n_op):
            acc = acc + az[use, j]
        return acc

    def share_plane(use, tiles):
        ap[use, s] = tiles
        return [
            send(ap.at[use, s], ap.at[use, s], ap_send.at[use, i], ap_recv.at[use, s], (other, z))
            for i, other in enumerate(plane)
        ]

    def add_plane(use):
        for other in plane:
            arrived(ap.at[use, other], ap_recv.at[use, other])
        acc = ap[use, 0]
        for j in range(1, n_sec):
            acc = acc + ap[use, j]
        return whole(acc[0:8]), whole(acc[8:16])

    def recur(k, block, where):
        value = block * weights[0] + basis[k - 1, where] * weights[1]
        if k > 1:
            value = value + basis[k - 2, where] * weights[2]
        return value

    weights = None
    last_inv = None
    alphas, betas = [], []
    for step in range(STEPS):
        g, nxt, use = step % 2, (step + 1) % 2, step % 2

        dot_acc = jnp.zeros((8, width), F32)
        rr = jnp.zeros((8, width), F32)
        rs = []
        for i, p in enumerate(order):
            inner = [None] * term_dev
            for c in range(3):
                x = gath[g][src[3 * i + c]].astype(F32)
                if step > 0:
                    x = recur(step, x, 3 * i + c)
                basis[step, 3 * i + c] = x
                terms = list(range(c, term_dev, 3))
                lhs = jnp.concatenate([left_v[p, t] for t in terms], axis=0)
                got = jnp.dot(lhs, x.astype(BF16), preferred_element_type=F32).astype(BF16)
                for n, t in enumerate(terms):
                    inner[t] = got[n * width:(n + 1) * width]
            part = jnp.dot(
                jnp.concatenate(inner, axis=1),
                right_v[p].reshape(term_dev * width, width),
                preferred_element_type=F32,
            )
            pb[p] = part.astype(BF16)
            dot_acc = dot_acc + fold(part * basis[step, 3 * i + own_c])
            if aligned and i < sec_dev - 1:
                rs.append(send(pb.at[p], rsb.at[z], rs_send.at[i], rs_recv.at[z], (s, p)))
        if not aligned:
            for i, mate in enumerate(mates):
                rs.append(send(chunk(pb, 0, mate), rsb.at[z], rs_send.at[i], rs_recv.at[z], (s, mate)))
        for p in range(sec_dev):
            i = lax.rem(p + 2 * sec_dev - 1 - z, sec_dev) if aligned else p
            own = basis[step, 3 * i + own_c]
            rr = rr + fold(own * own)
        az[use, z] = dot_acc
        small = share(use)
        rsb[z] = chunk(pb, 0, z)[...]
        for copy in sends:
            copy.wait_send()
        for mate in mates:
            arrived(rsb.at[mate], rs_recv.at[mate])
        image = rsb[0].astype(F32)
        for j in range(1, n_op):
            image = image + rsb[j].astype(F32)
        slot(nxt, s, z)[...] = (image * mask).astype(BF16)
        sends = spread_z(nxt)
        last = step == STEPS - 1
        if not last:
            sends += spread_plane(nxt, 0, z)
        small += share_plane(use, jnp.concatenate([add_op(use), rr], axis=0))
        if not last:
            for m, j in enumerate(mates):
                arrived(slot(nxt, s, j), rsem.at[nxt, s, j])
                sends += spread_plane(nxt, m + 1, j)
            sends += pass_on(nxt, 0, z)
        a_sum, n_sum = add_plane(use)
        norm = jnp.sqrt(n_sum / count + 1e-06)
        inv = 1.0 / norm
        alpha = a_sum * (scale / count) * inv * inv
        weights = [inv * scale, -alpha * inv]
        if step > 0:
            weights.append(-norm * last_inv)
            betas.append(norm)
        last_inv = inv
        alphas.append(alpha)
        if not last:
            for m, j in enumerate(mates):
                sends += pass_on(nxt, m + 1, j)
        for copy in rs + small:
            copy.wait_send()
        if not last:
            collect(nxt)

    g, use = STEPS % 2, STEPS % 2
    for mate in mates:
        arrived(slot(g, s, mate), rsem.at[g, s, mate])
    rr = jnp.zeros((8, width), F32)
    for i, p in enumerate(order):
        u = recur(STEPS, gath[g][s * sec_dev + p].astype(F32), 3 * i + own_c)
        theta_v[p] = u
        pb[p] = u.astype(BF16)
    for p in range(sec_dev):
        rr = rr + fold(theta_v[p] * theta_v[p])
    small = share_plane(use, jnp.concatenate([rr, rr], axis=0))
    for p in range(sec_dev):
        block = pb[p]
        dens_ref[p] = lax.dot_general(block, block, (((1,), (1,)), ((), ())), preferred_element_type=F32)
    _, n_sum = add_plane(use)
    norm = jnp.sqrt(n_sum / count + 1e-06)
    inv = 1.0 / norm
    betas.append(norm)
    for p in range(sec_dev):
        vec_ref[p] = theta_v[p] * inv
        dens_ref[p] = dens_ref[p] * (inv * inv * (1.0 / width))
    lane = lax.broadcasted_iota(jnp.int32, (8, 128), 1)
    coef = jnp.zeros((8, 128), F32)
    for i, value in enumerate(alphas + betas):
        coef = jnp.where(lane == i, value, coef)
    coef_ref[...] = coef
    for copy in sends + small:
        copy.wait_send()


def per_device(theta, left_env, right_env, perm, dims):
    sec_dev, width, _ = theta.shape
    term_dev = left_env.shape[1]
    n_sec, n_op = lax.axis_size("sector"), lax.axis_size("op")
    rows = sec_dev * width // n_op
    n_chip = n_sec // 2
    dma = pltpu.SemaphoreType.DMA
    vmem = pl.BlockSpec(memory_space=pltpu.VMEM)
    smem = pl.BlockSpec(memory_space=pltpu.SMEM)
    hbm = pl.BlockSpec(memory_space=pl.ANY)
    vec, coef, dens = pl.pallas_call(
        functools.partial(kernel, n_sec, n_op),
        out_shape=(
            jax.ShapeDtypeStruct(theta.shape, F32),
            jax.ShapeDtypeStruct((8, 128), F32),
            jax.ShapeDtypeStruct(theta.shape, F32),
        ),
        in_specs=[hbm, hbm, hbm, smem, smem],
        out_specs=(vmem, vmem, vmem),
        scratch_shapes=[
            pltpu.VMEM(theta.shape, F32),
            pltpu.VMEM(left_env.shape, BF16),
            pltpu.VMEM(right_env.shape, BF16),
            pltpu.VMEM((n_sec * sec_dev, width, width), BF16),
            pltpu.VMEM((n_sec * sec_dev, width, width), BF16),
            pltpu.VMEM((STEPS, 3 * sec_dev, width, width), F32),
            pltpu.VMEM((sec_dev, width, width), BF16),
            pltpu.VMEM((n_op, rows, width), BF16),
            pltpu.VMEM((2, n_op, 8, width), F32),
            pltpu.VMEM((2, n_sec, 16, width), F32),
            dma((3, sec_dev)),
            dma((2, n_sec, n_op)),
            dma((n_op,)),
            dma((n_op, n_chip)),
            dma((n_op, n_chip)),
            dma((n_op,)),
            dma((n_op,)),
            dma((n_op,)),
            dma((2, n_op)),
            dma((2, n_op)),
            dma((2, n_sec)),
            dma((2, n_sec)),
        ],
        compiler_params=pltpu.CompilerParams(
            collective_id=0, has_side_effects=True, vmem_limit_bytes=60 * 1024 * 1024
        ),
        cost_estimate=pl.CostEstimate(
            flops=STEPS * 4 * sec_dev * term_dev * width**3,
            bytes_accessed=4 * sec_dev * term_dev * width**2,
            transcendentals=0,
        ),
    )(theta, left_env, right_env, perm, dims)
    return vec, coef[0, :6], dens


def solution(mesh):
    placed = (
        P("sector", None, None),
        P("sector", "op", None, None),
        P("sector", "op", None, None),
        P(),
        P("sector", None),
    )
    return jax.shard_map(
        per_device,
        mesh=mesh,
        in_specs=placed,
        out_specs=(P("sector", None, None), P(), P("sector", None, None)),
        check_vma=False,
    )
```

```python
import functools

import jax
import jax.numpy as jnp
from jax import lax
from jax.experimental import pallas as pl
from jax.experimental.pallas import tpu as pltpu
from jax.sharding import PartitionSpec as P

MESH = pl.DeviceIdType.MESH
F32 = jnp.float32
BF16 = jnp.bfloat16
STEPS = 3


def kernel(
    n_sec, n_op,
    theta_hbm, left_hbm, right_hbm, perm_ref, dims_ref,
    vec_ref, coef_ref, dens_ref,
    theta_v, left_v, right_v, gath_a, gath_b, basis, pb, rsb, az, ap,
    env_sem, rsem, zsend, psend, fsend, zrecv, rs_send, rs_recv,
    az_send, az_recv, ap_send, ap_recv,
):
    gath = (gath_a, gath_b)
    sec_dev, width, _ = theta_v.shape
    term_dev = left_v.shape[1]
    total = n_sec * sec_dev
    count = float(total * width * width)
    scale = float((term_dev * n_op) ** -0.5)
    rows = sec_dev * width // n_op
    cpb = width // rows
    n_chip = n_sec // 2
    aligned = n_op == sec_dev
    rounds = ((0, 1), (1, n_op - 1))

    s = lax.axis_index("sector")
    z = lax.axis_index("op")
    core = lax.rem(s, 2)
    chip = s // 2
    sib = s + 1 - 2 * core
    beside = [lax.rem(chip + m, n_chip) for m in range(1, n_chip)]
    peers = [2 * c + core for c in beside]
    others = [sib] + [2 * c + 1 - core for c in beside]
    mates = [lax.rem(z + m, n_op) for m in range(1, n_op)]
    plane = [lax.rem(s + m, n_sec) for m in range(1, n_sec)]

    fetch = pltpu.make_async_copy(theta_hbm, theta_v, env_sem.at[2, 0])
    fetch.start()
    env = []
    for p in range(sec_dev):
        env.append(pltpu.make_async_copy(left_hbm.at[p], left_v.at[p], env_sem.at[0, p]))
        env.append(pltpu.make_async_copy(right_hbm.at[p], right_v.at[p], env_sem.at[1, p]))
    for copy in env:
        copy.start()

    barrier = pltpu.get_barrier_semaphore()
    for other in plane:
        pl.semaphore_signal(barrier, inc=1, device_id=(other, z), device_id_type=MESH)
    for other in mates:
        pl.semaphore_signal(barrier, inc=1, device_id=(s, other), device_id_type=MESH)

    def block_mask(p, first, n):
        r = lax.broadcasted_iota(jnp.int32, (n, width), 0) + first
        c = lax.broadcasted_iota(jnp.int32, (n, width), 1)
        return jnp.where((r < dims_ref[0, p]) & (c < dims_ref[1, p]), 1.0, 0.0).astype(F32)

    def chunk(ref, base, j):
        if cpb == 1:
            return ref.at[base + j]
        return ref.at[base + j // cpb, pl.ds(pl.multiple_of(lax.rem(j, cpb) * rows, rows), rows)]

    def slots(g, owner, part):
        first, n = rounds[part]
        return gath[g].at[pl.ds(owner * n_op + first, n)]

    def place(block):
        first = lax.rem(block, sec_dev) * cpb
        base = lax.div(block, sec_dev) * n_op
        return [base + lax.rem(first + h - z + n_op, n_op) for h in range(cpb)]

    def load(g, where):
        return jnp.concatenate([gath[g][w] for w in where], axis=0)

    def send(src, dst, ssem, dsem, dev):
        copy = pltpu.make_async_remote_copy(
            src_ref=src, dst_ref=dst, send_sem=ssem, recv_sem=dsem,
            device_id=dev, device_id_type=MESH,
        )
        copy.start()
        return copy

    def arrived(dst, dsem):
        pltpu.make_async_remote_copy(
            src_ref=dst, dst_ref=dst, send_sem=zsend.at[0], recv_sem=dsem,
            device_id=(sib, z), device_id_type=MESH,
        ).wait_recv()

    def fold(x):
        return jnp.sum(x.reshape(x.shape[0] // 8, 8, width), axis=0)

    def whole(x):
        return jnp.sum(x, keepdims=True)

    def move(g, owner, part, ssem, dev):
        ref = slots(g, owner, part)
        return send(ref, ref, ssem, rsem.at[g, owner, part], (dev, z))

    def spread_z(g):
        return [
            send(
                gath[g].at[s * n_op], gath[g].at[s * n_op + n_op - i],
                zsend.at[i - 1], zrecv.at[n_op - i], (s, mate),
            )
            for i, mate in enumerate(mates, 1)
        ]

    def collect_z(g):
        for m in range(1, n_op):
            arrived(gath[g].at[s * n_op + m], zrecv.at[m])

    def spread_plane(g, part):
        return [move(g, s, part, psend.at[part, i], dev) for i, dev in enumerate(peers + [sib])]

    def pass_on(g, part):
        out = []
        for i, peer in enumerate(peers):
            arrived(slots(g, peer, part), rsem.at[g, peer, part])
            out.append(move(g, peer, part, fsend.at[part, i], sib))
        return out

    def collect(g):
        for part in range(2):
            for other in others:
                arrived(slots(g, other, part), rsem.at[g, other, part])

    own_p = z // cpb
    own_r = pl.multiple_of(lax.rem(z, cpb) * rows, rows)
    fetch.wait()
    mask = block_mask(own_p, own_r, rows)
    for m in range(n_op):
        j = lax.rem(z + m, n_op)
        p, first = j // cpb, pl.multiple_of(lax.rem(j, cpb) * rows, rows)
        kept = theta_v[p, pl.ds(first, rows), :] * block_mask(p, first, rows)
        gath[0][s * n_op + m] = kept.astype(BF16)

    pl.semaphore_wait(barrier, n_sec - 1 + n_op - 1)

    sends = spread_plane(0, 0) + spread_plane(0, 1)

    order = [lax.rem(z + 1 + i, sec_dev) if aligned else i for i in range(sec_dev)]
    wants = []
    for p in order:
        mine = perm_ref[s * sec_dev + p]
        for c in range(3):
            q = lax.rem(z * term_dev + c, 3)
            wants.append(lax.rem(mine + q - 1 + total, total))
    own_c = lax.rem(3 * term_dev * n_op + 1 - z * term_dev, 3)

    def look(i, found):
        here = perm_ref[i]
        return tuple(jnp.where(here == w, i, f) for w, f in zip(wants, found))

    src = lax.fori_loop(0, total, look, tuple(jnp.int32(0) for _ in wants))

    src = [place(block) for block in src]
    sends += pass_on(0, 0) + pass_on(0, 1)
    collect(0)
    for copy in env:
        copy.wait()

    def share(use):
        return [
            send(az.at[use, z], az.at[use, z], az_send.at[use, i], az_recv.at[use, z], (s, mate))
            for i, mate in enumerate(mates)
        ]

    def add_op(use):
        for mate in mates:
            arrived(az.at[use, mate], az_recv.at[use, mate])
        acc = az[use, 0]
        for j in range(1, n_op):
            acc = acc + az[use, j]
        return acc

    def share_plane(use, tiles):
        ap[use, s] = tiles
        return [
            send(ap.at[use, s], ap.at[use, s], ap_send.at[use, i], ap_recv.at[use, s], (other, z))
            for i, other in enumerate(plane)
        ]

    def add_plane(use):
        for other in plane:
            arrived(ap.at[use, other], ap_recv.at[use, other])
        acc = ap[use, 0]
        for j in range(1, n_sec):
            acc = acc + ap[use, j]
        return whole(acc[0:8]), whole(acc[8:16])

    def recur(k, block, where):
        value = block * weights[0] + basis[k - 1, where] * weights[1]
        if k > 1:
            value = value + basis[k - 2, where] * weights[2]
        return value

    weights = None
    last_inv = None
    alphas, betas = [], []
    for step in range(STEPS):
        g, nxt, use = step % 2, (step + 1) % 2, step % 2

        dot_acc = jnp.zeros((8, width), F32)
        rr = jnp.zeros((8, width), F32)
        rs = []
        for i, p in enumerate(order):
            inner = [None] * term_dev
            for c in range(3):
                x = load(g, src[3 * i + c]).astype(F32)
                if step > 0:
                    x = recur(step, x, 3 * i + c)
                basis[step, 3 * i + c] = x
                terms = list(range(c, term_dev, 3))
                lhs = jnp.concatenate([left_v[p, t] for t in terms], axis=0)
                got = jnp.dot(lhs, x.astype(BF16), preferred_element_type=F32).astype(BF16)
                for n, t in enumerate(terms):
                    inner[t] = got[n * width:(n + 1) * width]
            part = jnp.dot(
                jnp.concatenate(inner, axis=1),
                right_v[p].reshape(term_dev * width, width),
                preferred_element_type=F32,
            )
            pb[p] = part.astype(BF16)
            dot_acc = dot_acc + fold(part * basis[step, 3 * i + own_c])
            if aligned and i < sec_dev - 1:
                rs.append(send(pb.at[p], rsb.at[z], rs_send.at[i], rs_recv.at[z], (s, p)))
        if not aligned:
            for i, mate in enumerate(mates):
                rs.append(send(chunk(pb, 0, mate), rsb.at[z], rs_send.at[i], rs_recv.at[z], (s, mate)))
        for p in range(sec_dev):
            i = lax.rem(p + 2 * sec_dev - 1 - z, sec_dev) if aligned else p
            own = basis[step, 3 * i + own_c]
            rr = rr + fold(own * own)
        az[use, z] = dot_acc
        small = share(use)
        rsb[z] = chunk(pb, 0, z)[...]
        for copy in sends:
            copy.wait_send()
        for mate in mates:
            arrived(rsb.at[mate], rs_recv.at[mate])
        image = rsb[0].astype(F32)
        for j in range(1, n_op):
            image = image + rsb[j].astype(F32)
        gath[nxt][s * n_op] = (image * mask).astype(BF16)
        sends = spread_z(nxt)
        last = step == STEPS - 1
        if not last:
            sends += spread_plane(nxt, 0)
        small += share_plane(use, jnp.concatenate([add_op(use), rr], axis=0))
        if not last:
            collect_z(nxt)
            sends += spread_plane(nxt, 1)
            sends += pass_on(nxt, 0)
        a_sum, n_sum = add_plane(use)
        norm = jnp.sqrt(n_sum / count + 1e-06)
        inv = 1.0 / norm
        alpha = a_sum * (scale / count) * inv * inv
        weights = [inv * scale, -alpha * inv]
        if step > 0:
            weights.append(-norm * last_inv)
            betas.append(norm)
        last_inv = inv
        alphas.append(alpha)
        if not last:
            sends += pass_on(nxt, 1)
        for copy in rs + small:
            copy.wait_send()
        if not last:
            collect(nxt)

    g, use = STEPS % 2, STEPS % 2
    collect_z(g)
    rr = jnp.zeros((8, width), F32)
    for i, p in enumerate(order):
        u = recur(STEPS, load(g, place(s * sec_dev + p)).astype(F32), 3 * i + own_c)
        theta_v[p] = u
        pb[p] = u.astype(BF16)
    for p in range(sec_dev):
        rr = rr + fold(theta_v[p] * theta_v[p])
    small = share_plane(use, jnp.concatenate([rr, rr], axis=0))
    for p in range(sec_dev):
        block = pb[p]
        dens_ref[p] = lax.dot_general(block, block, (((1,), (1,)), ((), ())), preferred_element_type=F32)
    _, n_sum = add_plane(use)
    norm = jnp.sqrt(n_sum / count + 1e-06)
    inv = 1.0 / norm
    betas.append(norm)
    for p in range(sec_dev):
        vec_ref[p] = theta_v[p] * inv
        dens_ref[p] = dens_ref[p] * (inv * inv * (1.0 / width))
    lane = lax.broadcasted_iota(jnp.int32, (8, 128), 1)
    coef = jnp.zeros((8, 128), F32)
    for i, value in enumerate(alphas + betas):
        coef = jnp.where(lane == i, value, coef)
    coef_ref[...] = coef
    for copy in sends + small:
        copy.wait_send()


def per_device(theta, left_env, right_env, perm, dims):
    sec_dev, width, _ = theta.shape
    term_dev = left_env.shape[1]
    n_sec, n_op = lax.axis_size("sector"), lax.axis_size("op")
    rows = sec_dev * width // n_op
    n_chip = n_sec // 2
    dma = pltpu.SemaphoreType.DMA
    vmem = pl.BlockSpec(memory_space=pltpu.VMEM)
    smem = pl.BlockSpec(memory_space=pltpu.SMEM)
    hbm = pl.BlockSpec(memory_space=pltpu.HBM)
    vec, coef, dens = pl.pallas_call(
        functools.partial(kernel, n_sec, n_op),
        out_shape=(
            jax.ShapeDtypeStruct(theta.shape, F32),
            jax.ShapeDtypeStruct((8, 128), F32),
            jax.ShapeDtypeStruct(theta.shape, F32),
        ),
        in_specs=[hbm, hbm, hbm, smem, smem],
        out_specs=(vmem, vmem, vmem),
        scratch_shapes=[
            pltpu.VMEM(theta.shape, F32),
            pltpu.VMEM(left_env.shape, BF16),
            pltpu.VMEM(right_env.shape, BF16),
            pltpu.VMEM((n_sec * n_op, rows, width), BF16),
            pltpu.VMEM((n_sec * n_op, rows, width), BF16),
            pltpu.VMEM((STEPS, 3 * sec_dev, width, width), F32),
            pltpu.VMEM((sec_dev, width, width), BF16),
            pltpu.VMEM((n_op, rows, width), BF16),
            pltpu.VMEM((2, n_op, 8, width), F32),
            pltpu.VMEM((2, n_sec, 16, width), F32),
            dma((3, sec_dev)),
            dma((2, n_sec, 2)),
            dma((n_op,)),
            dma((2, n_chip)),
            dma((2, n_chip)),
            dma((n_op,)),
            dma((n_op,)),
            dma((n_op,)),
            dma((2, n_op)),
            dma((2, n_op)),
            dma((2, n_sec)),
            dma((2, n_sec)),
        ],
        compiler_params=pltpu.CompilerParams(
            collective_id=0, has_side_effects=True, vmem_limit_bytes=53 * 1024 * 1024
        ),
        cost_estimate=pl.CostEstimate(
            flops=STEPS * 4 * sec_dev * term_dev * width**3,
            bytes_accessed=4 * sec_dev * term_dev * width**2,
            transcendentals=0,
        ),
    )(theta, left_env, right_env, perm, dims.T)
    return vec, coef[0, :6], dens


def solution(mesh):
    placed = (
        P("sector", None, None),
        P("sector", "op", None, None),
        P("sector", "op", None, None),
        P(),
        P("sector", None),
    )
    return jax.shard_map(
        per_device,
        mesh=mesh,
        in_specs=placed,
        out_specs=(P("sector", None, None), P(), P("sector", None, None)),
        check_vma=False,
    )
```

```python
import functools

import jax
import jax.numpy as jnp
from jax import lax
from jax.experimental import pallas as pl
from jax.experimental.pallas import tpu as pltpu
from jax.sharding import PartitionSpec as P

MESH = pl.DeviceIdType.MESH
F32 = jnp.float32
BF16 = jnp.bfloat16
STEPS = 3


def kernel(
    n_sec, n_op,
    theta_hbm, left_hbm, right_hbm, perm_ref, dims_ref,
    vec_ref, coef_ref, dens_ref,
    theta_v, left_v, right_v, gath_a, gath_b, basis, mid, pb, rsb, az, ap,
    env_sem, rsem, zsend, psend, fsend, zrecv, rs_send, rs_recv,
    az_send, az_recv, ap_send, ap_recv,
):
    gath = (gath_a, gath_b)
    sec_dev, width, _ = theta_v.shape
    term_dev = left_v.shape[1]
    total = n_sec * sec_dev
    count = float(total * width * width)
    scale = float((term_dev * n_op) ** -0.5)
    rows = sec_dev * width // n_op
    cpb = width // rows
    n_chip = n_sec // 2
    aligned = n_op == sec_dev
    rounds = ((0, 1), (1, n_op - 1))

    s = lax.axis_index("sector")
    z = lax.axis_index("op")
    core = lax.rem(s, 2)
    chip = s // 2
    sib = s + 1 - 2 * core
    beside = [lax.rem(chip + m, n_chip) for m in range(1, n_chip)]
    peers = [2 * c + core for c in beside]
    others = [sib] + [2 * c + 1 - core for c in beside]
    mates = [lax.rem(z + m, n_op) for m in range(1, n_op)]
    plane = [lax.rem(s + m, n_sec) for m in range(1, n_sec)]

    fetch = pltpu.make_async_copy(theta_hbm, theta_v, env_sem.at[2, 0])
    fetch.start()
    env = []
    for p in range(sec_dev):
        env.append(pltpu.make_async_copy(left_hbm.at[p], left_v.at[p], env_sem.at[0, p]))
        env.append(pltpu.make_async_copy(right_hbm.at[p], right_v.at[p], env_sem.at[1, p]))
    for copy in env:
        copy.start()

    barrier = pltpu.get_barrier_semaphore()
    for other in plane:
        pl.semaphore_signal(barrier, inc=1, device_id=(other, z), device_id_type=MESH)
    for other in mates:
        pl.semaphore_signal(barrier, inc=1, device_id=(s, other), device_id_type=MESH)

    def block_mask(p, first, n):
        r = lax.broadcasted_iota(jnp.int32, (n, width), 0) + first
        c = lax.broadcasted_iota(jnp.int32, (n, width), 1)
        return jnp.where((r < dims_ref[0, p]) & (c < dims_ref[1, p]), 1.0, 0.0).astype(F32)

    def chunk(ref, base, j):
        if cpb == 1:
            return ref.at[base + j]
        return ref.at[base + j // cpb, pl.ds(pl.multiple_of(lax.rem(j, cpb) * rows, rows), rows)]

    def slots(g, owner, part):
        first, n = rounds[part]
        return gath[g].at[pl.ds(owner * n_op + first, n)]

    def place(block):
        first = lax.rem(block, sec_dev) * cpb
        base = lax.div(block, sec_dev) * n_op
        return [base + lax.rem(first + h - z + n_op, n_op) for h in range(cpb)]

    def load(g, where):
        return jnp.concatenate([gath[g][w] for w in where], axis=0)

    def send(src, dst, ssem, dsem, dev):
        copy = pltpu.make_async_remote_copy(
            src_ref=src, dst_ref=dst, send_sem=ssem, recv_sem=dsem,
            device_id=dev, device_id_type=MESH,
        )
        copy.start()
        return copy

    def arrived(dst, dsem):
        pltpu.make_async_remote_copy(
            src_ref=dst, dst_ref=dst, send_sem=zsend.at[0], recv_sem=dsem,
            device_id=(sib, z), device_id_type=MESH,
        ).wait_recv()

    def fold(x):
        return jnp.sum(x.reshape(x.shape[0] // 8, 8, width), axis=0)

    def whole(x):
        return jnp.sum(x, keepdims=True)

    def move(g, owner, part, ssem, dev):
        ref = slots(g, owner, part)
        return send(ref, ref, ssem, rsem.at[g, owner, part], (dev, z))

    def spread_z(g):
        return [
            send(
                gath[g].at[s * n_op], gath[g].at[s * n_op + n_op - i],
                zsend.at[i - 1], zrecv.at[n_op - i], (s, mate),
            )
            for i, mate in enumerate(mates, 1)
        ]

    def collect_z(g):
        for m in range(1, n_op):
            arrived(gath[g].at[s * n_op + m], zrecv.at[m])

    def spread_plane(g, part):
        return [move(g, s, part, psend.at[part, i], dev) for i, dev in enumerate(peers + [sib])]

    def pass_on(g, part):
        out = []
        for i, peer in enumerate(peers):
            arrived(slots(g, peer, part), rsem.at[g, peer, part])
            out.append(move(g, peer, part, fsend.at[part, i], sib))
        return out

    def collect(g):
        for part in range(2):
            for other in others:
                arrived(slots(g, other, part), rsem.at[g, other, part])

    weights = []
    def recur(k, block, where):
        value = block * weights[-1][0] + basis[k - 1, where] * weights[-1][1]
        if k > 1:
            value = value + basis[k - 2, where] * weights[-1][2]
        return value

    per_class = term_dev // 3

    def own_place(p):
        return [s * n_op + lax.rem(p * cpb + h - z + n_op, n_op) for h in range(cpb)]

    def class_terms(q):
        first = lax.rem(3 * term_dev * n_op + q - z * term_dev, 3)
        return [first + 3 * n for n in range(per_class)]

    def left_products(p, terms, x):
        lhs = jnp.concatenate([left_v[p, t] for t in terms], axis=0)
        got = jnp.dot(lhs, x, preferred_element_type=F32).astype(BF16)
        return [got[n * width:(n + 1) * width] for n in range(len(terms))]

    def right_products(p, terms, inner):
        return jnp.dot(
            jnp.concatenate(inner, axis=1),
            jnp.concatenate([right_v[p, t] for t in terms], axis=0),
            preferred_element_type=F32,
        )

    def own_products(step, g):
        for i, p in enumerate(order):
            x = load(g, own_place(p)).astype(F32)
            if step > 0:
                x = recur(step, x, 3 * i + 1)
            basis[step, 3 * i + 1] = x
            terms = class_terms(1)
            mid[i] = right_products(p, terms, left_products(p, terms, x.astype(BF16)))

    own_p = z // cpb
    own_r = pl.multiple_of(lax.rem(z, cpb) * rows, rows)
    fetch.wait()
    mask = block_mask(own_p, own_r, rows)
    for m in range(n_op):
        j = lax.rem(z + m, n_op)
        p, first = j // cpb, pl.multiple_of(lax.rem(j, cpb) * rows, rows)
        kept = theta_v[p, pl.ds(first, rows), :] * block_mask(p, first, rows)
        gath[0][s * n_op + m] = kept.astype(BF16)

    pl.semaphore_wait(barrier, n_sec - 1 + n_op - 1)

    sends = spread_plane(0, 0) + spread_plane(0, 1)

    order = [lax.rem(z + 1 + i, sec_dev) if aligned else i for i in range(sec_dev)]
    wants = []
    for p in order:
        mine = perm_ref[s * sec_dev + p]
        wants += [lax.rem(mine + total - 1, total), lax.rem(mine + 1, total)]

    def look(i, found):
        here = perm_ref[i]
        return tuple(jnp.where(here == w, i, f) for w, f in zip(wants, found))

    src = lax.fori_loop(0, total, look, tuple(jnp.int32(0) for _ in wants))

    src = [place(block) for block in src]
    sends += pass_on(0, 0)
    for copy in env:
        copy.wait()
    own_products(0, 0)
    sends += pass_on(0, 1)
    collect(0)

    def share(use):
        return [
            send(az.at[use, z], az.at[use, z], az_send.at[use, i], az_recv.at[use, z], (s, mate))
            for i, mate in enumerate(mates)
        ]

    def add_op(use):
        for mate in mates:
            arrived(az.at[use, mate], az_recv.at[use, mate])
        acc = az[use, 0]
        for j in range(1, n_op):
            acc = acc + az[use, j]
        return acc

    def share_plane(use, tiles):
        ap[use, s] = tiles
        return [
            send(ap.at[use, s], ap.at[use, s], ap_send.at[use, i], ap_recv.at[use, s], (other, z))
            for i, other in enumerate(plane)
        ]

    def add_plane(use):
        for other in plane:
            arrived(ap.at[use, other], ap_recv.at[use, other])
        acc = ap[use, 0]
        for j in range(1, n_sec):
            acc = acc + ap[use, j]
        return whole(acc[0:8]), whole(acc[8:16])

    last_inv = None
    alphas, betas = [], []
    for step in range(STEPS):
        g, nxt, use = step % 2, (step + 1) % 2, step % 2

        dot_acc = jnp.zeros((8, width), F32)
        rr = jnp.zeros((8, width), F32)
        rs = []
        for i, p in enumerate(order):
            inner, terms = [], []
            for q in (0, 2):
                x = load(g, src[2 * i + q // 2]).astype(F32)
                if step > 0:
                    x = recur(step, x, 3 * i + q)
                basis[step, 3 * i + q] = x
                terms += class_terms(q)
                inner += left_products(p, class_terms(q), x.astype(BF16))
            for t in range(3 * per_class, term_dev):
                x = basis[step, 3 * i + lax.rem(z * term_dev + t, 3)]
                terms.append(t)
                inner += left_products(p, [t], x.astype(BF16))
            part = mid[i] + right_products(p, terms, inner)
            pb[p] = part.astype(BF16)
            dot_acc = dot_acc + fold(part * basis[step, 3 * i + 1])
            if aligned and i < sec_dev - 1:
                rs.append(send(pb.at[p], rsb.at[z], rs_send.at[i], rs_recv.at[z], (s, p)))
        if not aligned:
            for i, mate in enumerate(mates):
                rs.append(send(chunk(pb, 0, mate), rsb.at[z], rs_send.at[i], rs_recv.at[z], (s, mate)))
        for p in range(sec_dev):
            i = lax.rem(p + 2 * sec_dev - 1 - z, sec_dev) if aligned else p
            own = basis[step, 3 * i + 1]
            rr = rr + fold(own * own)
        az[use, z] = dot_acc
        small = share(use)
        rsb[z] = chunk(pb, 0, z)[...]
        for copy in sends:
            copy.wait_send()
        for mate in mates:
            arrived(rsb.at[mate], rs_recv.at[mate])
        image = rsb[0].astype(F32)
        for j in range(1, n_op):
            image = image + rsb[j].astype(F32)
        gath[nxt][s * n_op] = (image * mask).astype(BF16)
        sends = spread_z(nxt)
        last = step == STEPS - 1
        if not last:
            sends += spread_plane(nxt, 0)
        small += share_plane(use, jnp.concatenate([add_op(use), rr], axis=0))
        if not last:
            collect_z(nxt)
            sends += spread_plane(nxt, 1)
            sends += pass_on(nxt, 0)
        a_sum, n_sum = add_plane(use)
        norm = jnp.sqrt(n_sum / count + 1e-06)
        inv = 1.0 / norm
        alpha = a_sum * (scale / count) * inv * inv
        weights.append([inv * scale, -alpha * inv])
        if step > 0:
            weights[-1].append(-norm * last_inv)
            betas.append(norm)
        last_inv = inv
        alphas.append(alpha)
        if not last:
            own_products(step + 1, nxt)
            sends += pass_on(nxt, 1)
        for copy in rs + small:
            copy.wait_send()
        if not last:
            collect(nxt)

    g, use = STEPS % 2, STEPS % 2
    collect_z(g)
    rr = jnp.zeros((8, width), F32)
    for i, p in enumerate(order):
        u = recur(STEPS, load(g, own_place(p)).astype(F32), 3 * i + 1)
        theta_v[p] = u
        pb[p] = u.astype(BF16)
    for p in range(sec_dev):
        rr = rr + fold(theta_v[p] * theta_v[p])
    small = share_plane(use, jnp.concatenate([rr, rr], axis=0))
    for p in range(sec_dev):
        block = pb[p]
        dens_ref[p] = lax.dot_general(block, block, (((1,), (1,)), ((), ())), preferred_element_type=F32)
    _, n_sum = add_plane(use)
    norm = jnp.sqrt(n_sum / count + 1e-06)
    inv = 1.0 / norm
    betas.append(norm)
    for p in range(sec_dev):
        vec_ref[p] = theta_v[p] * inv
        dens_ref[p] = dens_ref[p] * (inv * inv * (1.0 / width))
    lane = lax.broadcasted_iota(jnp.int32, (8, 128), 1)
    coef = jnp.zeros((8, 128), F32)
    for i, value in enumerate(alphas + betas):
        coef = jnp.where(lane == i, value, coef)
    coef_ref[...] = coef
    for copy in sends + small:
        copy.wait_send()


def per_device(theta, left_env, right_env, perm, dims):
    sec_dev, width, _ = theta.shape
    term_dev = left_env.shape[1]
    n_sec, n_op = lax.axis_size("sector"), lax.axis_size("op")
    rows = sec_dev * width // n_op
    n_chip = n_sec // 2
    dma = pltpu.SemaphoreType.DMA
    vmem = pl.BlockSpec(memory_space=pltpu.VMEM)
    smem = pl.BlockSpec(memory_space=pltpu.SMEM)
    hbm = pl.BlockSpec(memory_space=pltpu.HBM)
    vec, coef, dens = pl.pallas_call(
        functools.partial(kernel, n_sec, n_op),
        out_shape=(
            jax.ShapeDtypeStruct(theta.shape, F32),
            jax.ShapeDtypeStruct((8, 128), F32),
            jax.ShapeDtypeStruct(theta.shape, F32),
        ),
        in_specs=[hbm, hbm, hbm, smem, smem],
        out_specs=(vmem, vmem, vmem),
        scratch_shapes=[
            pltpu.VMEM(theta.shape, F32),
            pltpu.VMEM(left_env.shape, BF16),
            pltpu.VMEM(right_env.shape, BF16),
            pltpu.VMEM((n_sec * n_op, rows, width), BF16),
            pltpu.VMEM((n_sec * n_op, rows, width), BF16),
            pltpu.VMEM((STEPS, 3 * sec_dev, width, width), F32),
            pltpu.VMEM((sec_dev, width, width), F32),
            pltpu.VMEM((sec_dev, width, width), BF16),
            pltpu.VMEM((n_op, rows, width), BF16),
            pltpu.VMEM((2, n_op, 8, width), F32),
            pltpu.VMEM((2, n_sec, 16, width), F32),
            dma((3, sec_dev)),
            dma((2, n_sec, 2)),
            dma((n_op,)),
            dma((2, n_chip)),
            dma((2, n_chip)),
            dma((n_op,)),
            dma((n_op,)),
            dma((n_op,)),
            dma((2, n_op)),
            dma((2, n_op)),
            dma((2, n_sec)),
            dma((2, n_sec)),
        ],
        compiler_params=pltpu.CompilerParams(
            collective_id=0, has_side_effects=True, vmem_limit_bytes=53 * 1024 * 1024
        ),
        cost_estimate=pl.CostEstimate(
            flops=STEPS * 4 * sec_dev * term_dev * width**3,
            bytes_accessed=4 * sec_dev * term_dev * width**2,
            transcendentals=0,
        ),
    )(theta, left_env, right_env, perm, dims.T)
    return vec, coef[0, :6], dens


def solution(mesh):
    placed = (
        P("sector", None, None),
        P("sector", "op", None, None),
        P("sector", "op", None, None),
        P(),
        P("sector", None),
    )
    return jax.shard_map(
        per_device,
        mesh=mesh,
        in_specs=placed,
        out_specs=(P("sector", None, None), P(), P("sector", None, None)),
        check_vma=False,
    )
```

```python
import functools

import jax
import jax.numpy as jnp
from jax import lax
from jax.experimental import pallas as pl
from jax.experimental.pallas import tpu as pltpu
from jax.sharding import PartitionSpec as P

MESH = pl.DeviceIdType.MESH
F32 = jnp.float32
BF16 = jnp.bfloat16
STEPS = 3


def kernel(
    n_sec, n_op,
    theta_hbm, left_hbm, right_hbm, perm_ref, dims_ref,
    vec_ref, coef_ref, dens_ref,
    theta_v, left_v, right_v, gath_a, gath_b, basis, mid, pb, rsb, az, ap,
    env_sem, rsem, zsend, psend, fsend, zrecv, rs_send, rs_recv,
    az_send, az_recv, ap_send, ap_recv,
):
    gath = (gath_a, gath_b)
    sec_dev, width, _ = theta_v.shape
    term_dev = left_v.shape[1]
    total = n_sec * sec_dev
    count = float(total * width * width)
    scale = float((term_dev * n_op) ** -0.5)
    rows = sec_dev * width // n_op
    cpb = width // rows
    n_chip = n_sec // 2
    aligned = n_op == sec_dev
    groups = ((0, n_op - 1), (n_op - 1, 1))

    def xor(a, b):
        out = 0
        for k in range(n_op.bit_length() - 1):
            bit = 1 << k
            out = out + bit * lax.rem(lax.div(a, bit) + (b // bit if isinstance(b, int) else lax.div(b, bit)), 2)
        return out

    s = lax.axis_index("sector")
    z = lax.axis_index("op")
    core = lax.rem(s, 2)
    chip = s // 2
    sib = s + 1 - 2 * core
    beside = [lax.rem(chip + m, n_chip) for m in range(1, n_chip)]
    peers = [2 * c + core for c in beside]
    others = [sib] + [2 * c + 1 - core for c in beside]
    mates = [xor(z, m) for m in range(1, n_op)]
    plane = [lax.rem(s + m, n_sec) for m in range(1, n_sec)]

    fetch = pltpu.make_async_copy(theta_hbm, theta_v, env_sem.at[2, 0])
    fetch.start()
    env = []
    for p in range(sec_dev):
        env.append(pltpu.make_async_copy(left_hbm.at[p], left_v.at[p], env_sem.at[0, p]))
        env.append(pltpu.make_async_copy(right_hbm.at[p], right_v.at[p], env_sem.at[1, p]))
    for copy in env:
        copy.start()

    barrier = pltpu.get_barrier_semaphore()
    for other in plane:
        pl.semaphore_signal(barrier, inc=1, device_id=(other, z), device_id_type=MESH)
    for other in mates:
        pl.semaphore_signal(barrier, inc=1, device_id=(s, other), device_id_type=MESH)

    def block_mask(p, first, n):
        r = lax.broadcasted_iota(jnp.int32, (n, width), 0) + first
        c = lax.broadcasted_iota(jnp.int32, (n, width), 1)
        return jnp.where((r < dims_ref[0, p]) & (c < dims_ref[1, p]), 1.0, 0.0).astype(F32)

    def chunk(ref, base, j):
        if cpb == 1:
            return ref.at[base + j]
        return ref.at[base + j // cpb, pl.ds(pl.multiple_of(lax.rem(j, cpb) * rows, rows), rows)]

    def slots(g, owner, first, n):
        return gath[g].at[pl.ds(owner * n_op + first, n)]

    def place(block):
        first = lax.rem(block, sec_dev) * cpb
        base = lax.div(block, sec_dev) * n_op
        return [base + xor(z, first + h) for h in range(cpb)]

    def load(g, where):
        return jnp.concatenate([gath[g][w] for w in where], axis=0)

    def send(src, dst, ssem, dsem, dev):
        copy = pltpu.make_async_remote_copy(
            src_ref=src, dst_ref=dst, send_sem=ssem, recv_sem=dsem,
            device_id=dev, device_id_type=MESH,
        )
        copy.start()
        return copy

    def arrived(dst, dsem):
        pltpu.make_async_remote_copy(
            src_ref=dst, dst_ref=dst, send_sem=zsend.at[0], recv_sem=dsem,
            device_id=(sib, z), device_id_type=MESH,
        ).wait_recv()

    def fold(x):
        return jnp.sum(x.reshape(x.shape[0] // 8, 8, width), axis=0)

    def whole(x):
        return jnp.sum(x, keepdims=True)

    def move(g, owner, span, ssem, k, dev):
        ref = slots(g, owner, *span)
        return send(ref, ref, ssem, rsem.at[g, owner, k], (dev, z))

    def spread_z(g):
        return [
            send(gath[g].at[s * n_op], gath[g].at[s * n_op + m], zsend.at[m], zrecv.at[m], (s, mate))
            for m, mate in enumerate(mates, 1)
        ]

    def collect_z(g, m):
        arrived(gath[g].at[s * n_op + m], zrecv.at[m])

    def spread_plane(g, span, k):
        return [move(g, s, span, psend.at[k, i], k, peer) for i, peer in enumerate(peers)]

    def spread_chip(g, k):
        return [move(g, s, groups[k], psend.at[k, n_chip - 1], k, sib)]

    def pass_on(g, k, spans):
        out = []
        for i, peer in enumerate(peers):
            for j, span in spans:
                arrived(slots(g, peer, *span), rsem.at[g, peer, j])
            out.append(move(g, peer, groups[k], fsend.at[k, i], k, sib))
        return out

    def collect(g):
        for k in range(2):
            for other in others:
                arrived(slots(g, other, *groups[k]), rsem.at[g, other, k])

    weights = []
    def recur(k, block, where):
        value = block * weights[-1][0] + basis[k - 1, where] * weights[-1][1]
        if k > 1:
            value = value + basis[k - 2, where] * weights[-1][2]
        return value

    per_class = term_dev // 3

    def own_place(p):
        return [s * n_op + xor(z, p * cpb + h) for h in range(cpb)]

    def class_terms(q):
        first = lax.rem(3 * term_dev * n_op + q - z * term_dev, 3)
        return [first + 3 * n for n in range(per_class)]

    def left_products(p, terms, x):
        lhs = jnp.concatenate([left_v[p, t] for t in terms], axis=0)
        got = jnp.dot(lhs, x, preferred_element_type=F32).astype(BF16)
        return [got[n * width:(n + 1) * width] for n in range(len(terms))]

    def right_products(p, terms, inner):
        return jnp.dot(
            jnp.concatenate(inner, axis=1),
            jnp.concatenate([right_v[p, t] for t in terms], axis=0),
            preferred_element_type=F32,
        )

    def own_products(step, g):
        for i, p in enumerate(order):
            x = load(g, own_place(p)).astype(F32)
            if step > 0:
                x = recur(step, x, 3 * i + 1)
            basis[step, 3 * i + 1] = x
            terms = class_terms(1)
            mid[i] = right_products(p, terms, left_products(p, terms, x.astype(BF16)))

    own_p = z // cpb
    own_r = pl.multiple_of(lax.rem(z, cpb) * rows, rows)
    fetch.wait()
    mask = block_mask(own_p, own_r, rows)
    for m in range(n_op):
        j = xor(z, m)
        p, first = lax.div(j, cpb), pl.multiple_of(lax.rem(j, cpb) * rows, rows)
        kept = theta_v[p, pl.ds(first, rows), :] * block_mask(p, first, rows)
        gath[0][s * n_op + m] = kept.astype(BF16)

    pl.semaphore_wait(barrier, n_sec - 1 + n_op - 1)

    sends = []
    for k in range(2):
        sends += spread_plane(0, groups[k], k) + spread_chip(0, k)

    order = [xor(z, sec_dev - 1 - i) if aligned else i for i in range(sec_dev)]
    wants = []
    for p in order:
        mine = perm_ref[s * sec_dev + p]
        wants += [lax.rem(mine + total - 1, total), lax.rem(mine + 1, total)]

    def look(i, found):
        here = perm_ref[i]
        return tuple(jnp.where(here == w, i, f) for w, f in zip(wants, found))

    src = lax.fori_loop(0, total, look, tuple(jnp.int32(0) for _ in wants))

    src = [place(block) for block in src]
    for k in range(2):
        sends += pass_on(0, k, [(k, groups[k])])
    for copy in env:
        copy.wait()
    own_products(0, 0)
    collect(0)

    def share(use):
        return [
            send(az.at[use, z], az.at[use, z], az_send.at[use, i], az_recv.at[use, z], (s, mate))
            for i, mate in enumerate(mates)
        ]

    def add_op(use):
        for mate in mates:
            arrived(az.at[use, mate], az_recv.at[use, mate])
        acc = az[use, 0]
        for j in range(1, n_op):
            acc = acc + az[use, j]
        return acc

    def share_plane(use, tiles):
        ap[use, s] = tiles
        return [
            send(ap.at[use, s], ap.at[use, s], ap_send.at[use, i], ap_recv.at[use, s], (other, z))
            for i, other in enumerate(plane)
        ]

    def add_plane(use):
        for other in plane:
            arrived(ap.at[use, other], ap_recv.at[use, other])
        acc = ap[use, 0]
        for j in range(1, n_sec):
            acc = acc + ap[use, j]
        return whole(acc[0:8]), whole(acc[8:16])

    last_inv = None
    alphas, betas = [], []
    for step in range(STEPS):
        g, nxt, use = step % 2, (step + 1) % 2, step % 2

        dot_acc = jnp.zeros((8, width), F32)
        rr = jnp.zeros((8, width), F32)
        rs = []
        for i, p in enumerate(order):
            inner, terms = [], []
            for q in (0, 2):
                x = load(g, src[2 * i + q // 2]).astype(F32)
                if step > 0:
                    x = recur(step, x, 3 * i + q)
                basis[step, 3 * i + q] = x
                terms += class_terms(q)
                inner += left_products(p, class_terms(q), x.astype(BF16))
            for t in range(3 * per_class, term_dev):
                x = basis[step, 3 * i + lax.rem(z * term_dev + t, 3)]
                terms.append(t)
                inner += left_products(p, [t], x.astype(BF16))
            part = mid[i] + right_products(p, terms, inner)
            pb[p] = part.astype(BF16)
            dot_acc = dot_acc + fold(part * basis[step, 3 * i + 1])
            if aligned and i < sec_dev - 1:
                rs.append(send(pb.at[p], rsb.at[z], rs_send.at[i], rs_recv.at[z], (s, p)))
        if not aligned:
            for i, mate in enumerate(mates):
                rs.append(send(chunk(pb, 0, mate), rsb.at[z], rs_send.at[i], rs_recv.at[z], (s, mate)))
        for p in range(sec_dev):
            i = sec_dev - 1 - xor(z, p) if aligned else p
            own = basis[step, 3 * i + 1]
            rr = rr + fold(own * own)
        az[use, z] = dot_acc
        small = share(use)
        rsb[z] = chunk(pb, 0, z)[...]
        for copy in sends:
            copy.wait_send()
        for mate in mates:
            arrived(rsb.at[mate], rs_recv.at[mate])
        image = rsb[0].astype(F32)
        for j in range(1, n_op):
            image = image + rsb[j].astype(F32)
        gath[nxt][s * n_op] = (image * mask).astype(BF16)
        sends = spread_z(nxt)
        last = step == STEPS - 1
        if not last:
            sends += spread_plane(nxt, (0, 1), 0)
        small += share_plane(use, jnp.concatenate([add_op(use), rr], axis=0))
        if not last:
            for m in range(1, n_op):
                collect_z(nxt, m)
                sends += spread_plane(nxt, (m, 1), m)
                if m >= n_op - 2:
                    sends += spread_chip(nxt, m - n_op + 2)
            sends += pass_on(nxt, 0, [(m, (m, 1)) for m in range(n_op - 1)])
        a_sum, n_sum = add_plane(use)
        norm = jnp.sqrt(n_sum / count + 1e-06)
        inv = 1.0 / norm
        alpha = a_sum * (scale / count) * inv * inv
        weights.append([inv * scale, -alpha * inv])
        if step > 0:
            weights[-1].append(-norm * last_inv)
            betas.append(norm)
        last_inv = inv
        alphas.append(alpha)
        if not last:
            sends += pass_on(nxt, 1, [(n_op - 1, (n_op - 1, 1))])
            own_products(step + 1, nxt)
        for copy in rs + small:
            copy.wait_send()
        if not last:
            collect(nxt)

    g, use = STEPS % 2, STEPS % 2
    for m in range(1, n_op):
        collect_z(g, m)
    rr = jnp.zeros((8, width), F32)
    for i, p in enumerate(order):
        u = recur(STEPS, load(g, own_place(p)).astype(F32), 3 * i + 1)
        theta_v[p] = u
        pb[p] = u.astype(BF16)
    for p in range(sec_dev):
        rr = rr + fold(theta_v[p] * theta_v[p])
    small = share_plane(use, jnp.concatenate([rr, rr], axis=0))
    for p in range(sec_dev):
        block = pb[p]
        dens_ref[p] = lax.dot_general(block, block, (((1,), (1,)), ((), ())), preferred_element_type=F32)
    _, n_sum = add_plane(use)
    norm = jnp.sqrt(n_sum / count + 1e-06)
    inv = 1.0 / norm
    betas.append(norm)
    for p in range(sec_dev):
        vec_ref[p] = theta_v[p] * inv
        dens_ref[p] = dens_ref[p] * (inv * inv * (1.0 / width))
    lane = lax.broadcasted_iota(jnp.int32, (8, 128), 1)
    coef = jnp.zeros((8, 128), F32)
    for i, value in enumerate(alphas + betas):
        coef = jnp.where(lane == i, value, coef)
    coef_ref[...] = coef
    for copy in sends + small:
        copy.wait_send()


def per_device(theta, left_env, right_env, perm, dims):
    sec_dev, width, _ = theta.shape
    term_dev = left_env.shape[1]
    n_sec, n_op = lax.axis_size("sector"), lax.axis_size("op")
    rows = sec_dev * width // n_op
    n_chip = n_sec // 2
    dma = pltpu.SemaphoreType.DMA
    vmem = pl.BlockSpec(memory_space=pltpu.VMEM)
    smem = pl.BlockSpec(memory_space=pltpu.SMEM)
    hbm = pl.BlockSpec(memory_space=pltpu.HBM)
    vec, coef, dens = pl.pallas_call(
        functools.partial(kernel, n_sec, n_op),
        out_shape=(
            jax.ShapeDtypeStruct(theta.shape, F32),
            jax.ShapeDtypeStruct((8, 128), F32),
            jax.ShapeDtypeStruct(theta.shape, F32),
        ),
        in_specs=[hbm, hbm, hbm, smem, smem],
        out_specs=(vmem, vmem, vmem),
        scratch_shapes=[
            pltpu.VMEM(theta.shape, F32),
            pltpu.VMEM(left_env.shape, BF16),
            pltpu.VMEM(right_env.shape, BF16),
            pltpu.VMEM((n_sec * n_op, rows, width), BF16),
            pltpu.VMEM((n_sec * n_op, rows, width), BF16),
            pltpu.VMEM((STEPS, 3 * sec_dev, width, width), F32),
            pltpu.VMEM((sec_dev, width, width), F32),
            pltpu.VMEM((sec_dev, width, width), BF16),
            pltpu.VMEM((n_op, rows, width), BF16),
            pltpu.VMEM((2, n_op, 8, width), F32),
            pltpu.VMEM((2, n_sec, 16, width), F32),
            dma((3, sec_dev)),
            dma((2, n_sec, n_op)),
            dma((n_op,)),
            dma((n_op, n_chip)),
            dma((2, n_chip)),
            dma((n_op,)),
            dma((n_op,)),
            dma((n_op,)),
            dma((2, n_op)),
            dma((2, n_op)),
            dma((2, n_sec)),
            dma((2, n_sec)),
        ],
        compiler_params=pltpu.CompilerParams(
            collective_id=0, has_side_effects=True, vmem_limit_bytes=54580 * 1024
        ),
        cost_estimate=pl.CostEstimate(
            flops=STEPS * 4 * sec_dev * term_dev * width**3,
            bytes_accessed=4 * sec_dev * term_dev * width**2,
            transcendentals=0,
        ),
    )(theta, left_env, right_env, perm, dims.T)
    return vec, coef[0, :6], dens


def solution(mesh):
    placed = (
        P("sector", None, None),
        P("sector", "op", None, None),
        P("sector", "op", None, None),
        P(),
        P("sector", None),
    )
    return jax.shard_map(
        per_device,
        mesh=mesh,
        in_specs=placed,
        out_specs=(P("sector", None, None), P(), P("sector", None, None)),
        check_vma=False,
    )
```

```python
import functools

import jax
import jax.numpy as jnp
from jax import lax
from jax.experimental import pallas as pl
from jax.experimental.pallas import tpu as pltpu
from jax.sharding import PartitionSpec as P

MESH = pl.DeviceIdType.MESH
F32 = jnp.float32
BF16 = jnp.bfloat16
STEPS = 3


def kernel(
    n_sec, n_op,
    theta_hbm, left_hbm, right_hbm, perm_ref, dims_ref,
    vec_ref, coef_ref, dens_ref,
    theta_v, left_v, right_v, gath_a, gath_b, basis, mid, pb, rsb, az, ap,
    env_sem, rsem, zsend, psend, fsend, zrecv, pass_sem, rs_send, rs_recv,
    az_send, az_recv, ap_send, ap_recv,
):
    gath = (gath_a, gath_b)
    sec_dev, width, _ = theta_v.shape
    term_dev = left_v.shape[1]
    total = n_sec * sec_dev
    count = float(total * width * width)
    scale = float((term_dev * n_op) ** -0.5)
    rows = sec_dev * width // n_op
    cpb = width // rows
    n_chip = n_sec // 2
    aligned = n_op == sec_dev
    half = n_op // 2
    groups = ((0, half), (half, n_op - half))
    square = n_chip == 4

    def xor(a, b):
        out = 0
        for k in range(n_op.bit_length() - 1):
            bit = 1 << k
            out = out + bit * lax.rem(lax.div(a, bit) + (b // bit if isinstance(b, int) else lax.div(b, bit)), 2)
        return out

    s = lax.axis_index("sector")
    z = lax.axis_index("op")
    core = lax.rem(s, 2)
    chip = s // 2
    sib = s + 1 - 2 * core
    if square:
        beside = [chip + 1 - 2 * lax.rem(chip, 2), lax.rem(chip + 2, 4), 3 - chip]
    else:
        beside = [lax.rem(chip + m, n_chip) for m in range(1, n_chip)]
    peers = [2 * c + core for c in beside]
    near = [0, 1] if square else list(range(n_chip - 1))
    far = [2] if square else []
    others = [sib] + [2 * c + 1 - core for c in beside]
    mates = [xor(z, m) for m in range(1, n_op)]
    plane = [lax.rem(s + m, n_sec) for m in range(1, n_sec)]

    fetch = pltpu.make_async_copy(theta_hbm, theta_v, env_sem.at[2, 0])
    fetch.start()
    env = []
    for p in range(sec_dev):
        env.append(pltpu.make_async_copy(left_hbm.at[p], left_v.at[p], env_sem.at[0, p]))
        env.append(pltpu.make_async_copy(right_hbm.at[p], right_v.at[p], env_sem.at[1, p]))
    for copy in env:
        copy.start()

    barrier = pltpu.get_barrier_semaphore()
    for other in plane:
        pl.semaphore_signal(barrier, inc=1, device_id=(other, z), device_id_type=MESH)
    for other in mates:
        pl.semaphore_signal(barrier, inc=1, device_id=(s, other), device_id_type=MESH)

    def block_mask(p, first, n):
        r = lax.broadcasted_iota(jnp.int32, (n, width), 0) + first
        c = lax.broadcasted_iota(jnp.int32, (n, width), 1)
        return jnp.where((r < dims_ref[0, p]) & (c < dims_ref[1, p]), 1.0, 0.0).astype(F32)

    def chunk(ref, base, j):
        if cpb == 1:
            return ref.at[base + j]
        return ref.at[base + j // cpb, pl.ds(pl.multiple_of(lax.rem(j, cpb) * rows, rows), rows)]

    def slots(g, owner, first, n):
        return gath[g].at[pl.ds(owner * n_op + first, n)]

    def place(block):
        first = lax.rem(block, sec_dev) * cpb
        base = lax.div(block, sec_dev) * n_op
        return [base + xor(z, first + h) for h in range(cpb)]

    def load(g, where):
        return jnp.concatenate([gath[g][w] for w in where], axis=0)

    def send(src, dst, ssem, dsem, dev):
        copy = pltpu.make_async_remote_copy(
            src_ref=src, dst_ref=dst, send_sem=ssem, recv_sem=dsem,
            device_id=dev, device_id_type=MESH,
        )
        copy.start()
        return copy

    def arrived(dst, dsem):
        pltpu.make_async_remote_copy(
            src_ref=dst, dst_ref=dst, send_sem=zsend.at[0], recv_sem=dsem,
            device_id=(sib, z), device_id_type=MESH,
        ).wait_recv()

    def fold(x):
        return jnp.sum(x.reshape(x.shape[0] // 8, 8, width), axis=0)

    def whole(x):
        return jnp.sum(x, keepdims=True)

    def move(g, owner, span, ssem, k, dev):
        ref = slots(g, owner, *span)
        return send(ref, ref, ssem, rsem.at[g, owner, k], (dev, z))

    def spread_z(g):
        return [
            send(gath[g].at[s * n_op], gath[g].at[s * n_op + m], zsend.at[m], zrecv.at[m], (s, mate))
            for m, mate in enumerate(mates, 1)
        ]

    def collect_z(g, m):
        arrived(gath[g].at[s * n_op + m], zrecv.at[m])

    def spread_plane(g, span, k):
        return [move(g, s, span, psend.at[k, i], k, peers[i]) for i in near]

    def spread_chip(g, k):
        return [move(g, s, groups[k], psend.at[k, n_chip - 1], k, sib)]

    def take(g, i, j, span, done):
        if (i, j) not in done:
            done.add((i, j))
            arrived(slots(g, peers[i], *span), rsem.at[g, peers[i], j])

    def relay(g, j, first, span, done):
        if not square:
            return []
        i = 0 if first else 1
        take(g, i, j, span, done)
        return [move(g, peers[i], span, pass_sem.at[j], j, peers[1 - i])]

    def pass_on(g, k, who, spans, done):
        out = []
        for i in who:
            for j, span in spans:
                take(g, i, j, span, done)
            out.append(move(g, peers[i], groups[k], fsend.at[k, i], k, sib))
        return out

    def collect(g):
        for k in range(2):
            for other in others:
                arrived(slots(g, other, *groups[k]), rsem.at[g, other, k])

    weights = []
    def recur(k, block, where):
        value = block * weights[-1][0] + basis[k - 1, where] * weights[-1][1]
        if k > 1:
            value = value + basis[k - 2, where] * weights[-1][2]
        return value

    per_class = term_dev // 3

    def own_place(p):
        return [s * n_op + xor(z, p * cpb + h) for h in range(cpb)]

    def class_terms(q):
        first = lax.rem(3 * term_dev * n_op + q - z * term_dev, 3)
        return [first + 3 * n for n in range(per_class)]

    def left_products(p, terms, x):
        lhs = jnp.concatenate([left_v[p, t] for t in terms], axis=0)
        got = jnp.dot(lhs, x, preferred_element_type=F32).astype(BF16)
        return [got[n * width:(n + 1) * width] for n in range(len(terms))]

    def right_products(p, terms, inner):
        return jnp.dot(
            jnp.concatenate(inner, axis=1),
            jnp.concatenate([right_v[p, t] for t in terms], axis=0),
            preferred_element_type=F32,
        )

    def own_products(step, g):
        for i, p in enumerate(order):
            x = load(g, own_place(p)).astype(F32)
            if step > 0:
                x = recur(step, x, 3 * i + 1)
            basis[step, 3 * i + 1] = x
            terms = class_terms(1)
            mid[i] = right_products(p, terms, left_products(p, terms, x.astype(BF16)))

    own_p = z // cpb
    own_r = pl.multiple_of(lax.rem(z, cpb) * rows, rows)
    fetch.wait()
    mask = block_mask(own_p, own_r, rows)
    for m in range(n_op):
        j = xor(z, m)
        p, first = lax.div(j, cpb), pl.multiple_of(lax.rem(j, cpb) * rows, rows)
        kept = theta_v[p, pl.ds(first, rows), :] * block_mask(p, first, rows)
        gath[0][s * n_op + m] = kept.astype(BF16)

    pl.semaphore_wait(barrier, n_sec - 1 + n_op - 1)

    sends = []
    for k in range(2):
        sends += spread_plane(0, groups[k], k) + spread_chip(0, k)

    order = [xor(z, sec_dev - 1 - i) if aligned else i for i in range(sec_dev)]
    wants = []
    for p in order:
        mine = perm_ref[s * sec_dev + p]
        wants += [lax.rem(mine + total - 1, total), lax.rem(mine + 1, total)]

    def look(i, found):
        here = perm_ref[i]
        return tuple(jnp.where(here == w, i, f) for w, f in zip(wants, found))

    src = lax.fori_loop(0, total, look, tuple(jnp.int32(0) for _ in wants))

    src = [place(block) for block in src]
    done = set()
    for k in range(2):
        sends += relay(0, k, k == 0, groups[k], done)
    for who in (near, far):
        for k in range(2):
            sends += pass_on(0, k, who, [(k, groups[k])], done)
    for copy in env:
        copy.wait()
    own_products(0, 0)
    collect(0)

    def share(use):
        return [
            send(az.at[use, z], az.at[use, z], az_send.at[use, i], az_recv.at[use, z], (s, mate))
            for i, mate in enumerate(mates)
        ]

    def add_op(use):
        for mate in mates:
            arrived(az.at[use, mate], az_recv.at[use, mate])
        acc = az[use, 0]
        for j in range(1, n_op):
            acc = acc + az[use, j]
        return acc

    def share_plane(use, tiles):
        ap[use, s] = tiles
        return [
            send(ap.at[use, s], ap.at[use, s], ap_send.at[use, i], ap_recv.at[use, s], (other, z))
            for i, other in enumerate(plane)
        ]

    def add_plane(use):
        for other in plane:
            arrived(ap.at[use, other], ap_recv.at[use, other])
        acc = ap[use, 0]
        for j in range(1, n_sec):
            acc = acc + ap[use, j]
        return whole(acc[0:8]), whole(acc[8:16])

    last_inv = None
    alphas, betas = [], []
    for step in range(STEPS):
        g, nxt, use = step % 2, (step + 1) % 2, step % 2

        dot_acc = jnp.zeros((8, width), F32)
        rr = jnp.zeros((8, width), F32)
        rs = []
        for i, p in enumerate(order):
            inner, terms = [], []
            for q in (0, 2):
                x = load(g, src[2 * i + q // 2]).astype(F32)
                if step > 0:
                    x = recur(step, x, 3 * i + q)
                basis[step, 3 * i + q] = x
                terms += class_terms(q)
                inner += left_products(p, class_terms(q), x.astype(BF16))
            for t in range(3 * per_class, term_dev):
                x = basis[step, 3 * i + lax.rem(z * term_dev + t, 3)]
                terms.append(t)
                inner += left_products(p, [t], x.astype(BF16))
            part = mid[i] + right_products(p, terms, inner)
            pb[p] = part.astype(BF16)
            dot_acc = dot_acc + fold(part * basis[step, 3 * i + 1])
            if aligned and i < sec_dev - 1:
                rs.append(send(pb.at[p], rsb.at[z], rs_send.at[i], rs_recv.at[z], (s, p)))
        if not aligned:
            for i, mate in enumerate(mates):
                rs.append(send(chunk(pb, 0, mate), rsb.at[z], rs_send.at[i], rs_recv.at[z], (s, mate)))
        for p in range(sec_dev):
            i = sec_dev - 1 - xor(z, p) if aligned else p
            own = basis[step, 3 * i + 1]
            rr = rr + fold(own * own)
        az[use, z] = dot_acc
        small = share(use)
        rsb[z] = chunk(pb, 0, z)[...]
        for copy in sends:
            copy.wait_send()
        for mate in mates:
            arrived(rsb.at[mate], rs_recv.at[mate])
        image = rsb[0].astype(F32)
        for j in range(1, n_op):
            image = image + rsb[j].astype(F32)
        gath[nxt][s * n_op] = (image * mask).astype(BF16)
        sends = spread_z(nxt)
        last = step == STEPS - 1
        if not last:
            sends += spread_plane(nxt, (0, 1), 0)
        small += share_plane(use, jnp.concatenate([add_op(use), rr], axis=0))
        if not last:
            done = set()
            spans = [[(m, (m, 1)) for m in range(a, a + n)] for a, n in groups]
            for m in range(1, n_op):
                collect_z(nxt, m)
                sends += spread_plane(nxt, (m, 1), m)
                if m == half - 1 or m == n_op - 1:
                    sends += spread_chip(nxt, m // half)
                if m >= 2:
                    sends += relay(nxt, m - 2, m - 2 < half, (m - 2, 1), done)
            for m in range(n_op - 2, n_op):
                sends += relay(nxt, m, m < half, (m, 1), done)
            for k in range(2):
                sends += pass_on(nxt, k, near, spans[k], done)
        a_sum, n_sum = add_plane(use)
        norm = jnp.sqrt(n_sum / count + 1e-06)
        inv = 1.0 / norm
        alpha = a_sum * (scale / count) * inv * inv
        weights.append([inv * scale, -alpha * inv])
        if step > 0:
            weights[-1].append(-norm * last_inv)
            betas.append(norm)
        last_inv = inv
        alphas.append(alpha)
        if not last:
            for k in range(2):
                sends += pass_on(nxt, k, far, spans[k], done)
            own_products(step + 1, nxt)
        for copy in rs + small:
            copy.wait_send()
        if not last:
            collect(nxt)

    g, use = STEPS % 2, STEPS % 2
    for m in range(1, n_op):
        collect_z(g, m)
    rr = jnp.zeros((8, width), F32)
    for i, p in enumerate(order):
        u = recur(STEPS, load(g, own_place(p)).astype(F32), 3 * i + 1)
        theta_v[p] = u
        pb[p] = u.astype(BF16)
    for p in range(sec_dev):
        rr = rr + fold(theta_v[p] * theta_v[p])
    small = share_plane(use, jnp.concatenate([rr, rr], axis=0))
    for p in range(sec_dev):
        block = pb[p]
        dens_ref[p] = lax.dot_general(block, block, (((1,), (1,)), ((), ())), preferred_element_type=F32)
    _, n_sum = add_plane(use)
    norm = jnp.sqrt(n_sum / count + 1e-06)
    inv = 1.0 / norm
    betas.append(norm)
    for p in range(sec_dev):
        vec_ref[p] = theta_v[p] * inv
        dens_ref[p] = dens_ref[p] * (inv * inv * (1.0 / width))
    lane = lax.broadcasted_iota(jnp.int32, (8, 128), 1)
    coef = jnp.zeros((8, 128), F32)
    for i, value in enumerate(alphas + betas):
        coef = jnp.where(lane == i, value, coef)
    coef_ref[...] = coef
    for copy in sends + small:
        copy.wait_send()


def per_device(theta, left_env, right_env, perm, dims):
    sec_dev, width, _ = theta.shape
    term_dev = left_env.shape[1]
    n_sec, n_op = lax.axis_size("sector"), lax.axis_size("op")
    rows = sec_dev * width // n_op
    n_chip = n_sec // 2
    dma = pltpu.SemaphoreType.DMA
    vmem = pl.BlockSpec(memory_space=pltpu.VMEM)
    smem = pl.BlockSpec(memory_space=pltpu.SMEM)
    hbm = pl.BlockSpec(memory_space=pltpu.HBM)
    vec, coef, dens = pl.pallas_call(
        functools.partial(kernel, n_sec, n_op),
        out_shape=(
            jax.ShapeDtypeStruct(theta.shape, F32),
            jax.ShapeDtypeStruct((8, 128), F32),
            jax.ShapeDtypeStruct(theta.shape, F32),
        ),
        in_specs=[hbm, hbm, hbm, smem, smem],
        out_specs=(vmem, vmem, vmem),
        scratch_shapes=[
            pltpu.VMEM(theta.shape, F32),
            pltpu.VMEM(left_env.shape, BF16),
            pltpu.VMEM(right_env.shape, BF16),
            pltpu.VMEM((n_sec * n_op, rows, width), BF16),
            pltpu.VMEM((n_sec * n_op, rows, width), BF16),
            pltpu.VMEM((STEPS, 3 * sec_dev, width, width), F32),
            pltpu.VMEM((sec_dev, width, width), F32),
            pltpu.VMEM((sec_dev, width, width), BF16),
            pltpu.VMEM((n_op, rows, width), BF16),
            pltpu.VMEM((2, n_op, 8, width), F32),
            pltpu.VMEM((2, n_sec, 16, width), F32),
            dma((3, sec_dev)),
            dma((2, n_sec, n_op)),
            dma((n_op,)),
            dma((n_op, n_chip)),
            dma((2, n_chip)),
            dma((n_op,)),
            dma((n_op,)),
            dma((n_op,)),
            dma((n_op,)),
            dma((2, n_op)),
            dma((2, n_op)),
            dma((2, n_sec)),
            dma((2, n_sec)),
        ],
        compiler_params=pltpu.CompilerParams(
            collective_id=0, has_side_effects=True, vmem_limit_bytes=54580 * 1024
        ),
        cost_estimate=pl.CostEstimate(
            flops=STEPS * 4 * sec_dev * term_dev * width**3,
            bytes_accessed=4 * sec_dev * term_dev * width**2,
            transcendentals=0,
        ),
    )(theta, left_env, right_env, perm, dims.T)
    return vec, coef[0, :6], dens


def solution(mesh):
    placed = (
        P("sector", None, None),
        P("sector", "op", None, None),
        P("sector", "op", None, None),
        P(),
        P("sector", None),
    )
    return jax.shard_map(
        per_device,
        mesh=mesh,
        in_specs=placed,
        out_specs=(P("sector", None, None), P(), P("sector", None, None)),
        check_vma=False,
    )
```

```python
import functools

import jax
import jax.numpy as jnp
from jax import lax
from jax.experimental import pallas as pl
from jax.experimental.pallas import tpu as pltpu
from jax.sharding import PartitionSpec as P

MESH = pl.DeviceIdType.MESH
F32 = jnp.float32
BF16 = jnp.bfloat16
STEPS = 3


def kernel(
    n_sec, n_op,
    theta_hbm, left_hbm, right_hbm, perm_ref, dims_ref,
    vec_ref, coef_ref, dens_ref,
    theta_v, left_v, right_v, gath_a, gath_b, basis, mid, pb, rsb, az, ap,
    env_sem, rsem, zsend, psend, fsend, zrecv, rs_send, rs_recv,
    az_send, az_recv, ap_send, ap_recv,
):
    gath = (gath_a, gath_b)
    sec_dev, width, _ = theta_v.shape
    term_dev = left_v.shape[1]
    total = n_sec * sec_dev
    count = float(total * width * width)
    scale = float((term_dev * n_op) ** -0.5)
    rows = sec_dev * width // n_op
    cpb = width // rows
    n_chip = n_sec // 2
    aligned = n_op == sec_dev
    groups = ((0, n_op - 1), (n_op - 1, 1))

    def xor(a, b):
        out = 0
        for k in range(n_op.bit_length() - 1):
            bit = 1 << k
            out = out + bit * lax.rem(lax.div(a, bit) + (b // bit if isinstance(b, int) else lax.div(b, bit)), 2)
        return out

    s = lax.axis_index("sector")
    z = lax.axis_index("op")
    core = lax.rem(s, 2)
    chip = s // 2
    sib = s + 1 - 2 * core
    if n_chip == 4:
        beside = [chip + 1 - 2 * lax.rem(chip, 2), lax.rem(chip + 2, 4), 3 - chip]
    else:
        beside = [lax.rem(chip + m, n_chip) for m in range(1, n_chip)]
    peers = [2 * c + core for c in beside]
    others = [sib] + [2 * c + 1 - core for c in beside]
    mates = [xor(z, m) for m in range(1, n_op)]
    plane = [lax.rem(s + m, n_sec) for m in range(1, n_sec)]

    fetch = pltpu.make_async_copy(theta_hbm, theta_v, env_sem.at[2, 0])
    fetch.start()
    env = []
    for p in range(sec_dev):
        env.append(pltpu.make_async_copy(left_hbm.at[p], left_v.at[p], env_sem.at[0, p]))
        env.append(pltpu.make_async_copy(right_hbm.at[p], right_v.at[p], env_sem.at[1, p]))
    for copy in env:
        copy.start()

    barrier = pltpu.get_barrier_semaphore()
    for other in plane:
        pl.semaphore_signal(barrier, inc=1, device_id=(other, z), device_id_type=MESH)
    for other in mates:
        pl.semaphore_signal(barrier, inc=1, device_id=(s, other), device_id_type=MESH)

    def block_mask(p, first, n):
        r = lax.broadcasted_iota(jnp.int32, (n, width), 0) + first
        c = lax.broadcasted_iota(jnp.int32, (n, width), 1)
        return jnp.where((r < dims_ref[0, p]) & (c < dims_ref[1, p]), 1.0, 0.0).astype(F32)

    def chunk(ref, base, j):
        if cpb == 1:
            return ref.at[base + j]
        return ref.at[base + j // cpb, pl.ds(pl.multiple_of(lax.rem(j, cpb) * rows, rows), rows)]

    def slots(g, owner, first, n):
        return gath[g].at[pl.ds(owner * n_op + first, n)]

    def place(block):
        first = lax.rem(block, sec_dev) * cpb
        base = lax.div(block, sec_dev) * n_op
        return [base + xor(z, first + h) for h in range(cpb)]

    def load(g, where):
        return jnp.concatenate([gath[g][w] for w in where], axis=0)

    def send(src, dst, ssem, dsem, dev):
        copy = pltpu.make_async_remote_copy(
            src_ref=src, dst_ref=dst, send_sem=ssem, recv_sem=dsem,
            device_id=dev, device_id_type=MESH,
        )
        copy.start()
        return copy

    def arrived(dst, dsem):
        pltpu.make_async_remote_copy(
            src_ref=dst, dst_ref=dst, send_sem=zsend.at[0], recv_sem=dsem,
            device_id=(sib, z), device_id_type=MESH,
        ).wait_recv()

    def fold(x):
        return jnp.sum(x.reshape(x.shape[0] // 8, 8, width), axis=0)

    def whole(x):
        return jnp.sum(x, keepdims=True)

    def move(g, owner, span, ssem, k, dev):
        ref = slots(g, owner, *span)
        return send(ref, ref, ssem, rsem.at[g, owner, k], (dev, z))

    def spread_z(g):
        return [
            send(gath[g].at[s * n_op], gath[g].at[s * n_op + m], zsend.at[m], zrecv.at[m], (s, mate))
            for m, mate in enumerate(mates, 1)
        ]

    def collect_z(g, m):
        arrived(gath[g].at[s * n_op + m], zrecv.at[m])

    def spread_plane(g, span, k):
        return [move(g, s, span, psend.at[k, i], k, peer) for i, peer in reversed(list(enumerate(peers)))]

    def spread_chip(g, k):
        return [move(g, s, groups[k], psend.at[k, n_chip - 1], k, sib)]

    def pass_on(g, k, spans):
        out = []
        for i, peer in enumerate(peers):
            for j, span in spans:
                arrived(slots(g, peer, *span), rsem.at[g, peer, j])
            out.append(move(g, peer, groups[k], fsend.at[k, i], k, sib))
        return out

    def collect(g):
        for k in range(2):
            for other in others:
                arrived(slots(g, other, *groups[k]), rsem.at[g, other, k])

    weights = []
    def recur(k, block, where):
        value = block * weights[-1][0] + basis[k - 1, where] * weights[-1][1]
        if k > 1:
            value = value + basis[k - 2, where] * weights[-1][2]
        return value

    per_class = term_dev // 3

    def own_place(p):
        return [s * n_op + xor(z, p * cpb + h) for h in range(cpb)]

    def class_terms(q):
        first = lax.rem(3 * term_dev * n_op + q - z * term_dev, 3)
        return [first + 3 * n for n in range(per_class)]

    def left_products(p, terms, x):
        lhs = jnp.concatenate([left_v[p, t] for t in terms], axis=0)
        got = jnp.dot(lhs, x, preferred_element_type=F32).astype(BF16)
        return [got[n * width:(n + 1) * width] for n in range(len(terms))]

    def right_products(p, terms, inner):
        return jnp.dot(
            jnp.concatenate(inner, axis=1),
            jnp.concatenate([right_v[p, t] for t in terms], axis=0),
            preferred_element_type=F32,
        )

    def own_products(step, g):
        for i, p in enumerate(order):
            x = load(g, own_place(p)).astype(F32)
            if step > 0:
                x = recur(step, x, 3 * i + 1)
            basis[step, 3 * i + 1] = x
            terms = class_terms(1)
            mid[i] = right_products(p, terms, left_products(p, terms, x.astype(BF16)))

    own_p = z // cpb
    own_r = pl.multiple_of(lax.rem(z, cpb) * rows, rows)
    fetch.wait()
    mask = block_mask(own_p, own_r, rows)
    for m in range(n_op):
        j = xor(z, m)
        p, first = lax.div(j, cpb), pl.multiple_of(lax.rem(j, cpb) * rows, rows)
        kept = theta_v[p, pl.ds(first, rows), :] * block_mask(p, first, rows)
        gath[0][s * n_op + m] = kept.astype(BF16)

    pl.semaphore_wait(barrier, n_sec - 1 + n_op - 1)

    sends = []
    for k in range(2):
        sends += spread_plane(0, groups[k], k) + spread_chip(0, k)

    order = [xor(z, sec_dev - 1 - i) if aligned else i for i in range(sec_dev)]
    wants = []
    for p in order:
        mine = perm_ref[s * sec_dev + p]
        wants += [lax.rem(mine + total - 1, total), lax.rem(mine + 1, total)]

    def look(i, found):
        here = perm_ref[i]
        return tuple(jnp.where(here == w, i, f) for w, f in zip(wants, found))

    src = lax.fori_loop(0, total, look, tuple(jnp.int32(0) for _ in wants))

    src = [place(block) for block in src]
    for k in range(2):
        sends += pass_on(0, k, [(k, groups[k])])
    for copy in env:
        copy.wait()
    own_products(0, 0)
    collect(0)

    def share(use):
        return [
            send(az.at[use, z], az.at[use, z], az_send.at[use, i], az_recv.at[use, z], (s, mate))
            for i, mate in enumerate(mates)
        ]

    def add_op(use):
        for mate in mates:
            arrived(az.at[use, mate], az_recv.at[use, mate])
        acc = az[use, 0]
        for j in range(1, n_op):
            acc = acc + az[use, j]
        return acc

    def share_plane(use, tiles):
        ap[use, s] = tiles
        return [
            send(ap.at[use, s], ap.at[use, s], ap_send.at[use, i], ap_recv.at[use, s], (other, z))
            for i, other in enumerate(plane)
        ]

    def add_plane(use):
        for other in plane:
            arrived(ap.at[use, other], ap_recv.at[use, other])
        acc = ap[use, 0]
        for j in range(1, n_sec):
            acc = acc + ap[use, j]
        return whole(acc[0:8]), whole(acc[8:16])

    last_inv = None
    alphas, betas = [], []
    for step in range(STEPS):
        g, nxt, use = step % 2, (step + 1) % 2, step % 2

        dot_acc = jnp.zeros((8, width), F32)
        rr = jnp.zeros((8, width), F32)
        rs = []
        for i, p in enumerate(order):
            inner, terms = [], []
            for q in (0, 2):
                x = load(g, src[2 * i + q // 2]).astype(F32)
                if step > 0:
                    x = recur(step, x, 3 * i + q)
                basis[step, 3 * i + q] = x
                terms += class_terms(q)
                inner += left_products(p, class_terms(q), x.astype(BF16))
            for t in range(3 * per_class, term_dev):
                x = basis[step, 3 * i + lax.rem(z * term_dev + t, 3)]
                terms.append(t)
                inner += left_products(p, [t], x.astype(BF16))
            part = mid[i] + right_products(p, terms, inner)
            pb[p] = part.astype(BF16)
            dot_acc = dot_acc + fold(part * basis[step, 3 * i + 1])
            if aligned and i < sec_dev - 1:
                rs.append(send(pb.at[p], rsb.at[z], rs_send.at[i], rs_recv.at[z], (s, p)))
        if not aligned:
            for i, mate in enumerate(mates):
                rs.append(send(chunk(pb, 0, mate), rsb.at[z], rs_send.at[i], rs_recv.at[z], (s, mate)))
        az[use, z] = dot_acc
        small = share(use)
        rsb[z] = chunk(pb, 0, z)[...]
        for copy in sends:
            copy.wait_send()
        for mate in mates:
            arrived(rsb.at[mate], rs_recv.at[mate])
        image = rsb[0].astype(F32)
        for j in range(1, n_op):
            image = image + rsb[j].astype(F32)
        gath[nxt][s * n_op] = (image * mask).astype(BF16)
        sends = spread_z(nxt)
        last = step == STEPS - 1
        if not last:
            sends += spread_plane(nxt, (0, 1), 0)
        for p in range(sec_dev):
            i = sec_dev - 1 - xor(z, p) if aligned else p
            own = basis[step, 3 * i + 1]
            rr = rr + fold(own * own)
        small += share_plane(use, jnp.concatenate([add_op(use), rr], axis=0))
        if not last:
            for m in range(1, n_op):
                collect_z(nxt, m)
                sends += spread_plane(nxt, (m, 1), m)
                if m >= n_op - 2:
                    sends += spread_chip(nxt, m - n_op + 2)
            sends += pass_on(nxt, 0, [(m, (m, 1)) for m in range(n_op - 1)])
        a_sum, n_sum = add_plane(use)
        norm = jnp.sqrt(n_sum / count + 1e-06)
        inv = 1.0 / norm
        alpha = a_sum * (scale / count) * inv * inv
        weights.append([inv * scale, -alpha * inv])
        if step > 0:
            weights[-1].append(-norm * last_inv)
            betas.append(norm)
        last_inv = inv
        alphas.append(alpha)
        if not last:
            sends += pass_on(nxt, 1, [(n_op - 1, (n_op - 1, 1))])
            own_products(step + 1, nxt)
        for copy in rs + small:
            copy.wait_send()
        if not last:
            collect(nxt)

    g, use = STEPS % 2, STEPS % 2
    for m in range(1, n_op):
        collect_z(g, m)
    rr = jnp.zeros((8, width), F32)
    for i, p in enumerate(order):
        u = recur(STEPS, load(g, own_place(p)).astype(F32), 3 * i + 1)
        theta_v[p] = u
        pb[p] = u.astype(BF16)
    for p in range(sec_dev):
        rr = rr + fold(theta_v[p] * theta_v[p])
    small = share_plane(use, jnp.concatenate([rr, rr], axis=0))
    for p in range(sec_dev):
        block = pb[p]
        dens_ref[p] = lax.dot_general(block, block, (((1,), (1,)), ((), ())), preferred_element_type=F32)
    _, n_sum = add_plane(use)
    norm = jnp.sqrt(n_sum / count + 1e-06)
    inv = 1.0 / norm
    betas.append(norm)
    for p in range(sec_dev):
        vec_ref[p] = theta_v[p] * inv
        dens_ref[p] = dens_ref[p] * (inv * inv * (1.0 / width))
    lane = lax.broadcasted_iota(jnp.int32, (8, 128), 1)
    coef = jnp.zeros((8, 128), F32)
    for i, value in enumerate(alphas + betas):
        coef = jnp.where(lane == i, value, coef)
    coef_ref[...] = coef
    for copy in sends + small:
        copy.wait_send()


def per_device(theta, left_env, right_env, perm, dims):
    sec_dev, width, _ = theta.shape
    term_dev = left_env.shape[1]
    n_sec, n_op = lax.axis_size("sector"), lax.axis_size("op")
    rows = sec_dev * width // n_op
    n_chip = n_sec // 2
    dma = pltpu.SemaphoreType.DMA
    vmem = pl.BlockSpec(memory_space=pltpu.VMEM)
    smem = pl.BlockSpec(memory_space=pltpu.SMEM)
    hbm = pl.BlockSpec(memory_space=pltpu.HBM)
    vec, coef, dens = pl.pallas_call(
        functools.partial(kernel, n_sec, n_op),
        out_shape=(
            jax.ShapeDtypeStruct(theta.shape, F32),
            jax.ShapeDtypeStruct((8, 128), F32),
            jax.ShapeDtypeStruct(theta.shape, F32),
        ),
        in_specs=[hbm, hbm, hbm, smem, smem],
        out_specs=(vmem, vmem, vmem),
        scratch_shapes=[
            pltpu.VMEM(theta.shape, F32),
            pltpu.VMEM(left_env.shape, BF16),
            pltpu.VMEM(right_env.shape, BF16),
            pltpu.VMEM((n_sec * n_op, rows, width), BF16),
            pltpu.VMEM((n_sec * n_op, rows, width), BF16),
            pltpu.VMEM((STEPS, 3 * sec_dev, width, width), F32),
            pltpu.VMEM((sec_dev, width, width), F32),
            pltpu.VMEM((sec_dev, width, width), BF16),
            pltpu.VMEM((n_op, rows, width), BF16),
            pltpu.VMEM((2, n_op, 8, width), F32),
            pltpu.VMEM((2, n_sec, 16, width), F32),
            dma((3, sec_dev)),
            dma((2, n_sec, n_op)),
            dma((n_op,)),
            dma((n_op, n_chip)),
            dma((2, n_chip)),
            dma((n_op,)),
            dma((n_op,)),
            dma((n_op,)),
            dma((2, n_op)),
            dma((2, n_op)),
            dma((2, n_sec)),
            dma((2, n_sec)),
        ],
        compiler_params=pltpu.CompilerParams(
            collective_id=0, has_side_effects=True, vmem_limit_bytes=54580 * 1024
        ),
        cost_estimate=pl.CostEstimate(
            flops=STEPS * 4 * sec_dev * term_dev * width**3,
            bytes_accessed=4 * sec_dev * term_dev * width**2,
            transcendentals=0,
        ),
    )(theta, left_env, right_env, perm, dims.T)
    return vec, coef[0, :6], dens


def solution(mesh):
    placed = (
        P("sector", None, None),
        P("sector", "op", None, None),
        P("sector", "op", None, None),
        P(),
        P("sector", None),
    )
    return jax.shard_map(
        per_device,
        mesh=mesh,
        in_specs=placed,
        out_specs=(P("sector", None, None), P(), P("sector", None, None)),
        check_vma=False,
    )
```
